512 devices in a mesh: dp: 64 (over x, y, core), ctx: 8 (over z).
Axes of the slice: x: 4, y: 8, z: 8, core: 2. Of those that a mesh axis runs over, the one named last changes fastest.
Arguments:
- queries: bfloat16 [64, 1152, 2560], P('dp', 'ctx'), may hold values from -128 to 128
- keys: bfloat16 [64, 1152, 2560], P('dp', 'ctx'), may hold values from -6 to 6
- values: bfloat16 [64, 1152, 2560], P('dp', 'ctx'), may hold values from -6 to 6
- frame_ids: int32 [64, 1152], P('dp', 'ctx'), may hold values from 0 to 15, never falling along the last dimension, each value on 1 to 144 neighbouring positions
- out_grad: bfloat16 [64, 1152, 2560], P('dp', 'ctx'), may hold values from -6 to 6
- q_prev: bfloat16 [32, 2560], replicated, may hold values from -0.125 to 0.125
- error: bfloat16 [64, 2560, 2560], P('dp', 'ctx'), may hold values from -18 to 18
Outputs:
- basis: float32 [32, 2560], P(None, 'ctx')
- q_factor: float32 [32, 2560], replicated
The draws below stay inside these ranges and needn't reach their ends.
Inputs may be any that keep to these rules, and one draw needn't show every extreme that they name: `frame_ids`: frame numbers never fall along a clip; a frame holds at most 144 tokens.
All inputs are finite; a program needn't handle non-finite values.
Results may differ from the reference program's by a relative error of at most 0.015.
Values may be sent and summed in bfloat16 or wider, within the bound.
A program may use at most 128 MiB of HBM per device.

```python
import math
import jax
import jax.numpy as jnp
import numpy as np
from jax import lax

HEADS = 20
HEAD_DIM = 128
OUT_W = 2560
RANK = 32
TOK_DEV = 144
HD = 2560
SEQ = 1152
CLIPS = 64
FRAMES = 16
N_DP = 64


def shared_keys(key):
    return jnp.clip(jax.random.normal(key, (CLIPS, SEQ, HD), jnp.float32), -6.0, 6.0)


def draw_keys(key, part):
    base = shared_keys(key)
    return base.astype(jnp.bfloat16)


def draw_queries(key, part):
    key = jax.random.fold_in(key, 23)
    fresh = jnp.clip(jax.random.normal(key, (CLIPS, SEQ, HD), jnp.float32), -6.0, 6.0)
    return fresh.astype(jnp.bfloat16)


def steps_of(rng, extent, shards, least, high):
    loudness, own = 1.0, jax.random.fold_in(rng, 6)
    for dim, shards_of in shards:
        heights = jnp.exp(jax.random.uniform(jax.random.fold_in(own, dim), (shards_of,), jnp.float32, least / len(shards), high / len(shards)))
        loudness = loudness * jnp.repeat(heights, extent[dim] // shards_of).reshape([-1 if axis == dim else 1 for axis in range(len(extent))])
    return loudness


def length_profile(amount, total, bound, lean):
    loads = [(1 << 20) // math.isqrt(grade ** lean) + 1 for grade in range(2, amount + 1)]
    surplus, holding = total - bound - (amount - 1), [1] * (amount - 1)
    while surplus > 0:
        candidates = [i for i in range(amount - 1) if holding[i] < bound]
        pool, remaining = sum([loads[i] for i in candidates]), surplus
        for i in candidates:
            extra = min(bound - holding[i], max(1, remaining * loads[i] // pool), surplus)
            holding[i] = holding[i] + extra
            surplus = surplus - extra
    return np.array([bound] + holding)


def uneven(key, number_of, total, reach, lean):
    if number_of == 2:
        one = jax.random.randint(key, (), max(1, total - reach), min(reach, total - 1) + 1)
        return jnp.stack([one, total - one])
    sizes = jnp.asarray(length_profile(number_of, total, reach, lean), jnp.int32)
    twos = (number_of - 1) // 2
    source_of, sink = sizes[1:1 + 2 * twos:2], sizes[2:2 + 2 * twos:2]
    margin = jnp.minimum(source_of - 1, reach - sink)
    shifted = jax.random.randint(jax.random.fold_in(key, 1), (twos,), 0, 1 << 20) % (margin + 1)
    sizes = sizes.at[1:1 + 2 * twos:2].set(source_of - shifted).at[2:2 + 2 * twos:2].set(sink + shifted)
    return sizes[jax.random.permutation(jax.random.fold_in(key, 2), number_of)]


def gaussian(stream_key, extent, spread, most, split=(), dtype=jnp.bfloat16):
    drawn = jax.random.normal(stream_key, extent, jnp.float32) * spread
    if len(split) > 0:
        drawn = steps_of(stream_key, extent, split, -0.22, 0.18) * drawn
    return jnp.clip(drawn, min=-most, max=most).astype(dtype)


def setup_inputs(seed: int = 0) -> dict:
    splits = jax.random.split(jax.random.key(seed), 8)
    queries = draw_queries(jax.random.fold_in(splits[7], 71), 0)
    keys = draw_keys(jax.random.fold_in(splits[7], 71), 0)
    values = gaussian(splits[2], (CLIPS, SEQ, HD), 1.0, 6.0, ((0, 64), (1, 8)))
    frame_ids = jax.vmap(lambda own: jnp.searchsorted(jnp.cumsum(uneven(own, FRAMES, SEQ, TOK_DEV, 1)), jnp.arange(SEQ), side="right"))(jax.random.split(splits[3], CLIPS)).reshape((CLIPS, SEQ)).astype(jnp.int32)
    out_grad = gaussian(splits[4], (CLIPS, SEQ, OUT_W), 1.0, 6.0, ((0, 64), (1, 8)))
    q_prev = gaussian(splits[5], (RANK, OUT_W), OUT_W ** -0.5, 0.125)
    error = gaussian(splits[6], (CLIPS, HD, OUT_W), 3.0, 18.0, ((0, 64), (1, 8)))
    return dict(queries=queries, keys=keys, values=values, frame_ids=frame_ids, out_grad=out_grad, q_prev=q_prev, error=error)


def attend(query_rows, key_rows, value_rows, frames):
    count = query_rows.shape[0]
    query_heads = query_rows.reshape(count, HEADS, HEAD_DIM).astype(jnp.float32)
    key_heads = key_rows.reshape(count, HEADS, HEAD_DIM).astype(jnp.float32)
    value_heads = value_rows.reshape(count, HEADS, HEAD_DIM).astype(jnp.float32)
    scores = jnp.einsum('ihd,jhd->hij', query_heads, key_heads) / math.sqrt(HEAD_DIM)
    allowed = (frames[None, :] <= frames[:, None])[None]
    scores = jnp.where(allowed, scores, jnp.float32(-1e+30))
    rowmax = lax.optimization_barrier(jnp.max(scores, axis=-1, keepdims=True))
    expo = jnp.where(allowed, jnp.exp(scores - rowmax), jnp.float32(0.0))
    denom = lax.optimization_barrier(jnp.sum(expo, axis=-1))
    probs = expo.astype(jnp.bfloat16).astype(jnp.float32)
    mixed = jnp.einsum('hij,jhd->hid', probs, value_heads) / denom[..., None]
    return mixed.transpose(1, 0, 2).reshape(count, HD).astype(jnp.bfloat16)

def reference(queries, keys, values, frame_ids, out_grad, q_prev, error):
    attn = lax.map(lambda items: attend(*items), (queries, keys, values, frame_ids))

    def left_term(items):
        attn_rows, grad_rows, error_rows = items
        dy_proj = jnp.dot(q_prev.astype(jnp.float32), grad_rows.T.astype(jnp.float32), preferred_element_type=jnp.float32).astype(jnp.bfloat16)
        token_part = jnp.dot(dy_proj.astype(jnp.float32), attn_rows.astype(jnp.float32), preferred_element_type=jnp.float32)
        memory_part = jnp.dot(q_prev.astype(jnp.float32), error_rows.T.astype(jnp.float32), preferred_element_type=jnp.float32)
        return token_part + memory_part
    p_sum = lax.optimization_barrier(jnp.sum(lax.map(left_term, (attn, out_grad, error)), axis=0))
    gram_matrix = jnp.dot(p_sum, p_sum.T, precision=lax.Precision.HIGHEST)
    lower = jnp.linalg.cholesky(gram_matrix)
    unit_rows = jax.scipy.linalg.solve_triangular(lower, p_sum, lower=True)
    basis = unit_rows * math.sqrt(HD)
    unit_bf = unit_rows.astype(jnp.bfloat16)

    def right_term(items):
        attn_rows, grad_rows, error_rows = items
        a_proj = jnp.dot(unit_bf.astype(jnp.float32), attn_rows.T.astype(jnp.float32), preferred_element_type=jnp.float32).astype(jnp.bfloat16)
        token_part = jnp.dot(a_proj.astype(jnp.float32), grad_rows.astype(jnp.float32), preferred_element_type=jnp.float32)
        memory_part = jnp.dot(unit_bf.astype(jnp.float32), error_rows.astype(jnp.float32), preferred_element_type=jnp.float32)
        return token_part + memory_part
    q_factor = lax.optimization_barrier(jnp.sum(lax.map(right_term, (attn, out_grad, error)), axis=0)) / N_DP
    return (basis, q_factor)
```

```python
import functools
import math

import jax
import jax.numpy as jnp
from jax import lax
from jax.experimental import pallas as pl
from jax.experimental.pallas import tpu as pltpu
from jax.sharding import PartitionSpec as P

MESH = pl.DeviceIdType.MESH
F32, BF16 = jnp.float32, jnp.bfloat16
HD = 2560
TOK = 144
SEQ = 1152
NZ, NX, NY = 8, 4, 8
DEPTH = 128
ROWS = 320
BLOCK = 384
EXACT = lax.Precision.HIGHEST
SCALE = math.log2(math.e) / math.sqrt(DEPTH)
SPANS = ((0, 640), (384, 1024), (768, 1152))


def rows_by_rows(left, right, precision=None):
    return lax.dot_general(
        left, right, (((1,), (1,)), ((), ())), preferred_element_type=F32, precision=precision
    )


def kernel(
    q_in, k_in, v_in, fr_in, og_in, qp_in, er_in,
    basis, q_out,
    qkv, code, frames, dys, probs, attn, og, qp, er, mem, tok,
    cores, others, xs, ys, halves, psum, mfull, gram, grams, bsum, bs,
    part, send, got, cores2, xs2, ys2, parts,
    in_sem, recv, sent, step_recv, step_sent, tail_recv, tail_sent,
):
    dp, z = lax.axis_index("dp"), lax.axis_index("ctx")
    c, y, x = dp % 2, (dp // 2) % NY, dp // (2 * NY)
    zpar = z % 2
    par = (z + c) % 2
    mate = z + 1 - 2 * zpar
    ring = [(z + d) % NZ for d in range(1, NZ)]
    z_peers = [(dp, t) for t in ring]
    x_peers = [(((x + d) % NX) * 2 * NY + 2 * y + c, z) for d in range(1, NX)]
    y_peers = [(x * 2 * NY + 2 * ((y + d) % NY) + c, z) for d in range(1, NY)]
    core_peer = (dp + 1 - 2 * c, z)
    cross_peer = (dp + 1 - 2 * c, mate)

    def remote(src, dst, ssem, rsem, to):
        return pltpu.make_async_remote_copy(
            src_ref=src, dst_ref=dst, send_sem=ssem, recv_sem=rsem, device_id=to, device_id_type=MESH
        )

    def drain(ref, sem):
        pltpu.make_async_copy(ref, ref, sem).wait()

    loads = [
        pltpu.make_async_copy(src, dst, in_sem.at[i])
        for i, (src, dst) in enumerate(((og_in, og), (qp_in, qp), (er_in, er)))
    ]
    for load in loads:
        load.start()

    everyone = z_peers + x_peers + y_peers + [core_peer, cross_peer]
    barrier = pltpu.get_barrier_semaphore()
    for to in everyone:
        pl.semaphore_signal(barrier, inc=1, device_id=to, device_id_type=MESH)
    pl.semaphore_wait(barrier, len(everyone))

    own_rows = pl.ds(pl.multiple_of(z * TOK, 16), TOK)
    tensors = (k_in, q_in, v_in)

    def columns(slot, t):
        head = 5 * (t // 2) + (2 if slot == 0 else 3 * (t % 2) + slot - 1)
        return pl.ds(pl.multiple_of(head * DEPTH, DEPTH), DEPTH)

    def send_head(slot, steps):
        for i, src in enumerate(tensors):
            for d in steps:
                t = (z + d) % NZ
                source, target = src.at[:, columns(slot, t)], qkv.at[slot, i, own_rows]
                if d == 0:
                    pltpu.make_async_copy(source, target, recv.at[slot, i]).start()
                else:
                    remote(source, target, sent.at[slot, i], recv.at[slot, i], (dp, t)).start()

    pltpu.make_async_copy(fr_in, frames.at[z], step_recv.at[0, 5]).start()
    for to in z_peers:
        remote(fr_in, frames.at[z], tail_sent.at[0], step_recv.at[0, 5], to).start()

    @pl.when(par == 0)
    def _():
        send_head(0, (4, 2, 6, 0))

    @pl.when(par == 1)
    def _():
        send_head(0, (3, 5, 1, 7))

    loads[0].wait()
    loads[1].wait()
    dys[z] = rows_by_rows(qp[...], og[...]).astype(BF16)
    for to in z_peers:
        remote(dys.at[z], dys.at[z], tail_sent.at[1], tail_recv.at[1], to).start()
    order = (4, 3, 5, 2, 6, 1, 7, 0)
    send_head(1, order)
    send_head(2, order)

    loads[2].wait()
    head_row = pl.multiple_of(64 * zpar, 64)
    half_row = pl.multiple_of(256 * (1 - zpar), 64)
    mem[0] = jnp.zeros((32, DEPTH), F32)
    mem[0, :, 0:64] = rows_by_rows(qp[...], er[pl.ds(half_row, 64), :])
    for s in (1, 2):
        rows = pl.ds(pl.multiple_of(head_row + DEPTH * (s - 1), 64), DEPTH)
        mem[s] = rows_by_rows(qp[...], er[rows, :])
    tok[...] = jnp.zeros_like(tok)
    bsum[...] = jnp.zeros_like(bsum)
    gram[...] = jnp.zeros_like(gram)

    drain(frames, step_recv.at[0, 5])
    number = lax.broadcasted_iota(jnp.int32, (16, TOK), 0)
    place = (
        lax.broadcasted_iota(jnp.int32, (16, DEPTH), 0) == lax.broadcasted_iota(jnp.int32, (16, DEPTH), 1)
    ).astype(F32)
    for j in range(NZ):
        row = jnp.broadcast_to(frames[j], (16, TOK))
        for i, value in enumerate((jnp.where(row == number, 1.0, 0.0), jnp.where(row > number, -1e30, 0.0))):
            code[i, j * TOK : (j + 1) * TOK, :] = lax.dot_general(
                value, place, (((0,), (0,)), ((), ())), preferred_element_type=F32
            ).astype(BF16)
    drain(dys.at[0:7], tail_recv.at[1])

    lane = lax.broadcasted_iota(jnp.int32, (32, DEPTH), 1)

    def attend(s):
        drain(qkv.at[s, 0], recv.at[s, 0])
        drain(qkv.at[s, 1], recv.at[s, 1])
        for first, reach in SPANS:
            queries = jnp.concatenate([qkv[s, 1, first : first + BLOCK, :], code[0, first : first + BLOCK, :]], axis=1)
            keys = jnp.concatenate([qkv[s, 0, 0:reach, :], code[1, 0:reach, :]], axis=1)
            scores = rows_by_rows(queries, keys)
            top = jnp.max(scores, axis=1, keepdims=True)
            probs[first : first + BLOCK, 0:reach] = jnp.exp2((scores - top) * SCALE).astype(BF16)
        drain(qkv.at[s, 2], recv.at[s, 2])
        for first, reach in SPANS:
            values = jnp.concatenate([qkv[s, 2, 0:reach, :], jnp.ones((reach, DEPTH), BF16)], axis=1)
            mixed = jnp.dot(probs[first : first + BLOCK, 0:reach], values, preferred_element_type=F32)
            attn[s, first : first + BLOCK, :] = (mixed[:, 0:DEPTH] / mixed[:, DEPTH:]).astype(BF16)
        total = jnp.zeros((32, DEPTH), F32)
        for j in range(NZ):
            total += jnp.dot(dys[j], attn[s, j * TOK : (j + 1) * TOK, :], preferred_element_type=F32)
        tok[s] = total

    def add_b(s, rows):
        high = rows.astype(BF16)
        both = jnp.concatenate([high, (rows - high.astype(F32)).astype(BF16)], axis=0)
        for j in range(NZ):
            found = rows_by_rows(both, attn[s, j * TOK : (j + 1) * TOK, :])
            bsum[j] += found[0:32] + found[32:64]

    def head(s, carry):
        middle = s == 0

        @pl.when(jnp.logical_or(s > 0, par == 0))
        def _():
            attend(s)

        here = tok[s]
        turned = pltpu.roll(here, 64, 1)
        even = zpar == 0
        mine = jnp.where(lane < 64, jnp.where(even, here, turned), 0.0)
        cores[s, c] = mem[s] + jnp.where(middle, mine, here)

        @pl.when(jnp.logical_and(middle, par == 0))
        def _():
            others[1] = jnp.where(lane < 64, jnp.where(even, turned, here), 0.0)
            for t in (0, 1):
                remote(others.at[1], others.at[0], step_sent.at[0, 3], step_recv.at[0, 3], (dp - c + t, mate)).start()

        remote(cores.at[s, c], cores.at[s, c], step_sent.at[s, 0], step_recv.at[s, 0], core_peer).start()
        drain(cores.at[s, 0], step_recv.at[s, 0])
        xs[s, x] = cores[s, 0] + cores[s, 1]

        @pl.when(middle)
        def _():
            drain(others.at[0], step_recv.at[0, 3])
            xs[0, x] += others[0]

        for to in x_peers:
            remote(xs.at[s, x], xs.at[s, x], step_sent.at[s, 1], step_recv.at[s, 1], to).start()
        drain(xs.at[s, 0:3], step_recv.at[s, 1])
        ys[s, y] = (xs[s, 0] + xs[s, 1]) + (xs[s, 2] + xs[s, 3])
        for to in y_peers:
            remote(ys.at[s, y], ys.at[s, y], step_sent.at[s, 2], step_recv.at[s, 2], to).start()
        drain(ys.at[s, 0:7], step_recv.at[s, 2])
        rows = ys[s, 0]
        for j in range(1, NY):
            rows += ys[s, j]
        psum[s] = rows
        gram[:, 0:32] += rows_by_rows(rows, rows, EXACT)

        @pl.when(s == 2)
        def _():
            folded = gram[0:8]
            for j in range(1, 4):
                folded += pltpu.roll(gram[8 * j : 8 * j + 8], 32 * j, 1)
            grams[z] = folded
            for to in z_peers:
                remote(grams.at[z], grams.at[z], tail_sent.at[2], tail_recv.at[2], to).start()

        @pl.when(middle)
        def _():
            @pl.when(par == 1)
            def _():
                copy = remote(psum.at[0], halves, step_sent.at[0, 4], step_recv.at[0, 4], (dp, mate))
                copy.start()
                copy.wait_send()

            @pl.when(par == 0)
            def _():
                drain(halves, step_recv.at[0, 4])
                own, other = psum[0], halves[...]
                mfull[...] = jnp.where(even, own, other) + pltpu.roll(jnp.where(even, other, own), 64, 1)
                add_b(0, mfull[...])

        @pl.when(s > 0)
        def _():
            add_b(s, psum[s])

        return carry

    lax.fori_loop(0, 3, head, 0)

    for d in range(1, NZ):
        t = (z + d) % NZ
        remote(bsum.at[t], bs.at[z], tail_sent.at[3], tail_recv.at[3], (dp, t)).start()
    bs[z] = bsum[z]

    drain(grams.at[0:7], tail_recv.at[2])
    folded = grams[0]
    for j in range(1, NZ):
        folded += grams[j]
    line = lax.broadcasted_iota(jnp.int32, (32, DEPTH), 0)
    work = jnp.concatenate([folded] + [pltpu.roll(folded, DEPTH - 32 * j, 1) for j in range(1, 4)], axis=0)
    work = jnp.where(lane < 32, work, jnp.where(lane - 32 == line, 1.0, 0.0))
    for j in range(32):
        pivot = work[j : j + 1, j : j + 1]
        scale = 1.0 / jnp.sqrt(pivot)
        row = work[j : j + 1, :] * scale
        column = jnp.where(line[:, 0:1] > j, work[:, j : j + 1] * scale, 0.0)
        work = jnp.where(line == j, row, work - column * row)
    inverse = pltpu.roll(work, DEPTH - 32, 1)[:, 0:32]

    units = [jnp.dot(inverse, psum[s], preferred_element_type=F32, precision=EXACT) for s in range(3)]
    middle_unit, first_unit, second_unit = [unit * math.sqrt(HD) for unit in units]
    first_turned, second_turned = pltpu.roll(first_unit, 64, 1), pltpu.roll(second_unit, 64, 1)
    low, even = lane < 64, zpar == 0
    basis[:, 0:128] = jnp.where(even, first_unit, jnp.where(low, middle_unit, first_turned))
    basis[:, 128:256] = jnp.where(even, second_unit, jnp.where(low, first_turned, second_turned))
    basis[:, 256:384] = jnp.where(even, middle_unit, second_turned)

    wide = 640
    middle_bf, first_bf, second_bf = [unit.astype(BF16) for unit in units]
    for j in range(4):
        cols = slice(wide * j, wide * (j + 1))
        part[:, cols] = (
            jnp.dot(first_bf, er[pl.ds(head_row, DEPTH), cols], preferred_element_type=F32)
            + jnp.dot(second_bf, er[pl.ds(pl.multiple_of(head_row + DEPTH, 64), DEPTH), cols], preferred_element_type=F32)
            + jnp.dot(middle_bf[:, 0:64], er[pl.ds(half_row, 64), cols], preferred_element_type=F32)
        )

    drain(bs.at[0:7], tail_recv.at[3])
    summed = bs[0]
    for j in range(1, NZ):
        summed += bs[j]
    a_proj = jnp.dot(inverse, summed, preferred_element_type=F32, precision=EXACT).astype(BF16)
    for j in range(4):
        cols = slice(wide * j, wide * (j + 1))
        found = part[:, cols] + jnp.dot(a_proj, og[:, cols], preferred_element_type=F32)
        send[j] = found[0:16].astype(BF16)
        send[4 + j] = found[16:32].astype(BF16)

    for d in range(1, NZ):
        t = (z + d) % NZ
        remote(send.at[t], got.at[z], tail_sent.at[4], tail_recv.at[4], (dp, t)).start()
    got[z] = send[z]
    drain(got.at[0:7], tail_recv.at[4])
    total = got[0].astype(F32)
    for j in range(1, NZ):
        total += got[j].astype(F32)
    cores2[c] = total
    remote(cores2.at[c], cores2.at[c], tail_sent.at[5], tail_recv.at[5], core_peer).start()
    drain(cores2.at[0], tail_recv.at[5])
    xs2[x] = (cores2[0] + cores2[1]).astype(BF16)
    for to in x_peers:
        remote(xs2.at[x], xs2.at[x], tail_sent.at[6], tail_recv.at[6], to).start()
    drain(xs2.at[0:3], tail_recv.at[6])
    total = xs2[0].astype(F32)
    for j in range(1, NX):
        total += xs2[j].astype(F32)
    ys2[y] = total.astype(BF16)
    for to in y_peers:
        remote(ys2.at[y], ys2.at[y], tail_sent.at[7], tail_recv.at[7], to).start()
    drain(ys2.at[0:7], tail_recv.at[7])
    total = ys2[0].astype(F32)
    for j in range(1, NY):
        total += ys2[j].astype(F32)
    parts[z] = total.astype(BF16)
    for to in z_peers:
        remote(parts.at[z], parts.at[z], tail_sent.at[8], tail_recv.at[8], to).start()
    drain(parts.at[0:7], tail_recv.at[8])
    for j in range(NZ):
        r, g = j // 4, j % 4
        q_out[16 * r : 16 * r + 16, wide * g : wide * (g + 1)] = parts[j].astype(F32) * (1.0 / 64)

    for s in (1, 2):
        for i in range(3):
            drain(qkv.at[0, i, 0 : 7 * TOK], sent.at[s, i])

    @pl.when(par == 0)
    def _():
        for i in range(3):
            drain(qkv.at[0, i, 0 : 3 * TOK], sent.at[0, i])
        drain(others, step_sent.at[0, 3])

    @pl.when(par == 1)
    def _():
        for i in range(3):
            drain(qkv.at[0, i, 0 : 4 * TOK], sent.at[0, i])

    for s in range(3):
        drain(cores.at[s, 0], step_sent.at[s, 0])
        drain(xs.at[s, 0:3], step_sent.at[s, 1])
        drain(ys.at[s, 0:7], step_sent.at[s, 2])
    drain(frames.at[0:7], tail_sent.at[0])
    drain(dys.at[0:7], tail_sent.at[1])
    drain(grams.at[0:7], tail_sent.at[2])
    drain(bs.at[0:7], tail_sent.at[3])
    drain(got.at[0:7], tail_sent.at[4])
    drain(cores2.at[0], tail_sent.at[5])
    drain(xs2.at[0:3], tail_sent.at[6])
    drain(ys2.at[0:7], tail_sent.at[7])
    drain(parts.at[0:7], tail_sent.at[8])


def body(queries, keys, values, frame_ids, out_grad, q_prev, error):
    vmem, dma = pltpu.VMEM, pltpu.SemaphoreType.DMA
    basis, q_factor = pl.pallas_call(
        kernel,
        out_shape=(jax.ShapeDtypeStruct((32, 384), F32), jax.ShapeDtypeStruct((32, HD), F32)),
        in_specs=[pl.BlockSpec(memory_space=pl.ANY)] * 7,
        out_specs=(pl.BlockSpec(memory_space=vmem), pl.BlockSpec(memory_space=vmem)),
        scratch_shapes=[
            vmem((3, 3, SEQ, DEPTH), BF16),
            vmem((2, SEQ, DEPTH), BF16),
            vmem((NZ, 1, TOK), jnp.int32),
            vmem((NZ, 32, TOK), BF16),
            vmem((SEQ, SEQ), BF16),
            vmem((3, SEQ, DEPTH), BF16),
            vmem((TOK, HD), BF16),
            vmem((32, HD), BF16),
            vmem((ROWS, HD), BF16),
            vmem((3, 32, DEPTH), F32),
            vmem((3, 32, DEPTH), F32),
            vmem((3, 2, 32, DEPTH), F32),
            vmem((2, 32, DEPTH), F32),
            vmem((3, NX, 32, DEPTH), F32),
            vmem((3, NY, 32, DEPTH), F32),
            vmem((32, DEPTH), F32),
            vmem((3, 32, DEPTH), F32),
            vmem((32, DEPTH), F32),
            vmem((32, DEPTH), F32),
            vmem((NZ, 8, DEPTH), F32),
            vmem((NZ, 32, TOK), F32),
            vmem((NZ, 32, TOK), F32),
            vmem((32, HD), F32),
            vmem((NZ, 16, 640), BF16),
            vmem((NZ, 16, 640), BF16),
            vmem((2, 16, 640), F32),
            vmem((NX, 16, 640), BF16),
            vmem((NY, 16, 640), BF16),
            vmem((NZ, 16, 640), BF16),
            dma((3,)),
            dma((3, 3)),
            dma((3, 3)),
            dma((3, 6)),
            dma((3, 6)),
            dma((9,)),
            dma((9,)),
        ],
        compiler_params=pltpu.CompilerParams(
            collective_id=0, has_side_effects=True, vmem_limit_bytes=56 * 1024 * 1024
        ),
    )(queries[0], keys[0], values[0], frame_ids, out_grad[0], q_prev, error[0])
    return (basis[:, 0:ROWS], q_factor)


def solution(mesh):
    placed = (
        P("dp", "ctx", None),
        P("dp", "ctx", None),
        P("dp", "ctx", None),
        P("dp", "ctx"),
        P("dp", "ctx", None),
        P(),
        P("dp", "ctx", None),
    )
    return jax.shard_map(
        body, mesh=mesh, in_specs=placed, out_specs=(P(None, "ctx"), P()), check_vma=False
    )
```

```python
import functools
import math

import jax
import jax.numpy as jnp
from jax import lax
from jax.experimental import pallas as pl
from jax.experimental.pallas import tpu as pltpu
from jax.sharding import PartitionSpec as P

MESH = pl.DeviceIdType.MESH
F32, BF16 = jnp.float32, jnp.bfloat16
HD = 2560
TOK = 144
SEQ = 1152
NZ, NX, NY = 8, 4, 8
DEPTH = 128
ROWS = 320
BLOCK = 384
EXACT = lax.Precision.HIGHEST
SCALE = math.log2(math.e) / math.sqrt(DEPTH)
SPANS = ((0, 640), (384, 1024), (768, 1152))


def rows_by_rows(left, right, precision=None):
    return lax.dot_general(
        left, right, (((1,), (1,)), ((), ())), preferred_element_type=F32, precision=precision
    )


def kernel(
    q_in, k_in, v_in, fr_in, og_in, qp_in, er_in,
    basis, q_out,
    qkv, code, frames, dys, probs, attn, og, qp, er, mem, tok,
    cores, others, xs, ys, halves, psum, gram, grams, bsum, bpack, bs,
    part, send, got, cores2, xs2, ys2,
    in_sem, recv, sent, step_recv, step_sent, tail_recv, tail_sent,
):
    dp, z = lax.axis_index("dp"), lax.axis_index("ctx")
    c, y, x = dp % 2, (dp // 2) % NY, dp // (2 * NY)
    zpar = z % 2
    par = (z + c) % 2
    mate = z + 1 - 2 * zpar
    even = zpar == 0
    far = (4, 3, 5, 2, 6, 1, 7)
    z_peers = [(dp, (z + d) % NZ) for d in far]
    x_peers = [(((x + d) % NX) * 2 * NY + 2 * y + c, z) for d in (2, 1, 3)]
    y_peers = [(x * 2 * NY + 2 * ((y + d) % NY) + c, z) for d in far]
    core_peer = (dp + 1 - 2 * c, z)
    cross_peer = (dp + 1 - 2 * c, mate)

    def remote(src, dst, ssem, rsem, to):
        return pltpu.make_async_remote_copy(
            src_ref=src, dst_ref=dst, send_sem=ssem, recv_sem=rsem, device_id=to, device_id_type=MESH
        )

    def drain(ref, sem):
        pltpu.make_async_copy(ref, ref, sem).wait()

    loads = [
        pltpu.make_async_copy(src, dst, in_sem.at[i])
        for i, (src, dst) in enumerate(((og_in, og), (qp_in, qp), (er_in, er)))
    ]
    for load in loads:
        load.start()

    everyone = z_peers + x_peers + y_peers + [core_peer, cross_peer]
    barrier = pltpu.get_barrier_semaphore()
    for to in everyone:
        pl.semaphore_signal(barrier, inc=1, device_id=to, device_id_type=MESH)
    pl.semaphore_wait(barrier, len(everyone))

    own_rows = pl.ds(pl.multiple_of(z * TOK, 16), TOK)
    tensors = (k_in, q_in, v_in)

    def columns(slot, t):
        head = 5 * (t // 2) + (2 if slot == 0 else 3 * (t % 2) + slot - 1)
        return pl.ds(pl.multiple_of(head * DEPTH, DEPTH), DEPTH)

    def send_to(slot, i, steps):
        for d in steps:
            t = (z + d) % NZ
            source, target = tensors[i].at[:, columns(slot, t)], qkv.at[slot, i, own_rows]
            if d == 0:
                pltpu.make_async_copy(source, target, recv.at[slot, i]).start()
            else:
                remote(source, target, sent.at[slot, i], recv.at[slot, i], (dp, t)).start()

    def send_head(slot, i):
        if slot > 0:
            send_to(slot, i, far + (0,))
            return

        @pl.when(par == 0)
        def _():
            send_to(0, i, (4, 2, 6, 0))

        @pl.when(par == 1)
        def _():
            send_to(0, i, (3, 5, 1, 7))

    def left(slot, i):
        if slot > 0:
            drain(qkv.at[0, i, 0 : 7 * TOK], sent.at[slot, i])
            return

        @pl.when(par == 0)
        def _():
            drain(qkv.at[0, i, 0 : 3 * TOK], sent.at[0, i])

        @pl.when(par == 1)
        def _():
            drain(qkv.at[0, i, 0 : 4 * TOK], sent.at[0, i])

    pltpu.make_async_copy(fr_in, frames.at[z], step_recv.at[5]).start()
    for to in z_peers:
        remote(fr_in, frames.at[z], tail_sent.at[0], step_recv.at[5], to).start()

    for i in range(3):
        send_head(0, i)

    loads[0].wait()
    loads[1].wait()
    dys[z] = rows_by_rows(qp[...], og[...]).astype(BF16)
    for to in z_peers:
        remote(dys.at[z], dys.at[z], tail_sent.at[1], tail_recv.at[1], to).start()
    send_head(1, 0)

    loads[2].wait()
    head_row = pl.multiple_of(64 * zpar, 64)
    half_row = pl.multiple_of(256 * (1 - zpar), 64)
    halves[...] = jnp.zeros((32, DEPTH), F32)
    halves[:, 0:64] = rows_by_rows(qp[...], er[pl.ds(half_row, 64), :])
    mine = halves[...]
    mem[0] = jnp.where(even, mine, pltpu.roll(mine, 64, 1))
    remote(mem.at[0], others.at[0], step_sent.at[4], step_recv.at[4], (dp, mate)).start()
    for s in (1, 2):
        rows = pl.ds(pl.multiple_of(head_row + DEPTH * (s - 1), 64), DEPTH)
        mem[s] = rows_by_rows(qp[...], er[rows, :])
    tok[...] = jnp.zeros_like(tok)
    bsum[...] = jnp.zeros_like(bsum)
    bpack[...] = jnp.zeros_like(bpack)
    gram[...] = jnp.zeros_like(gram)

    drain(frames, step_recv.at[5])
    number = lax.broadcasted_iota(jnp.int32, (16, TOK), 0)
    place = (
        lax.broadcasted_iota(jnp.int32, (16, DEPTH), 0) == lax.broadcasted_iota(jnp.int32, (16, DEPTH), 1)
    ).astype(F32)
    for j in range(NZ):
        row = jnp.broadcast_to(frames[j], (16, TOK))
        for i, value in enumerate((jnp.where(row == number, 1.0, 0.0), jnp.where(row > number, -1e30, 0.0))):
            code[i, j * TOK : (j + 1) * TOK, :] = lax.dot_general(
                value, place, (((0,), (0,)), ((), ())), preferred_element_type=F32
            ).astype(BF16)
    drain(dys.at[0:7], tail_recv.at[1])

    lane = lax.broadcasted_iota(jnp.int32, (32, DEPTH), 1)

    def attend(s):
        drain(qkv.at[s, 0], recv.at[s, 0])
        drain(qkv.at[s, 1], recv.at[s, 1])
        for first, reach in SPANS:
            queries = jnp.concatenate([qkv[s, 1, first : first + BLOCK, :], code[0, first : first + BLOCK, :]], axis=1)
            keys = jnp.concatenate([qkv[s, 0, 0:reach, :], code[1, 0:reach, :]], axis=1)
            scores = rows_by_rows(queries, keys)
            top = jnp.max(scores, axis=1, keepdims=True)
            probs[first : first + BLOCK, 0:reach] = jnp.exp2((scores - top) * SCALE).astype(BF16)
        drain(qkv.at[s, 2], recv.at[s, 2])
        for first, reach in SPANS:
            values = jnp.concatenate([qkv[s, 2, 0:reach, :], jnp.ones((reach, DEPTH), BF16)], axis=1)
            mixed = jnp.dot(probs[first : first + BLOCK, 0:reach], values, preferred_element_type=F32)
            attn[s, first : first + BLOCK, :] = (mixed[:, 0:DEPTH] / mixed[:, DEPTH:]).astype(BF16)
        total = jnp.zeros((32, DEPTH), F32)
        for j in range(NZ):
            total += jnp.dot(dys[j], attn[s, j * TOK : (j + 1) * TOK, :], preferred_element_type=F32)
        tok[s] = total

    def add_b(s, rows):
        high = rows.astype(BF16)
        both = jnp.concatenate([high, (rows - high.astype(F32)).astype(BF16)], axis=0)
        for j in range(NZ):
            found = rows_by_rows(both, attn[s, j * TOK : (j + 1) * TOK, :])
            bsum[j] += found[0:32] + found[32:64]

    def head(s, carry):
        @pl.when(s == 0)
        def _():
            for i, ahead in enumerate(((1, 1), (1, 2), (2, 0))):
                left(0, i)
                send_head(*ahead)

        @pl.when(s == 1)
        def _():
            for i, ahead in enumerate(((2, 1), (2, 2))):
                left(1, i)
                send_head(*ahead)

        @pl.when(jnp.logical_or(s > 0, par == 0))
        def _():
            attend(s)

        here = tok[s]
        cores[c, s] = mem[s] + here

        @pl.when(jnp.logical_and(s == 0, par == 0))
        def _():
            for t in (0, 1):
                remote(tok.at[0], others.at[1], step_sent.at[3], step_recv.at[3], (dp - c + t, mate)).start()

        return carry

    lax.fori_loop(0, 3, head, 0)

    drain(others.at[0], step_recv.at[4])
    cores[c, 0] += others[0]
    remote(cores.at[c], cores.at[c], step_sent.at[0], step_recv.at[0], core_peer).start()
    drain(others.at[1], step_recv.at[3])
    drain(cores.at[0], step_recv.at[0])
    total = cores[0] + cores[1]
    xs[x] = total.astype(BF16)
    xs[x, 0] = (total[0] + others[1]).astype(BF16)
    for to in x_peers:
        remote(xs.at[x], xs.at[x], step_sent.at[1], step_recv.at[1], to).start()
    drain(xs.at[0:3], step_recv.at[1])
    total = xs[0].astype(F32)
    for j in range(1, NX):
        total += xs[j].astype(F32)
    ys[y] = total.astype(BF16)
    for to in y_peers:
        remote(ys.at[y], ys.at[y], step_sent.at[2], step_recv.at[2], to).start()
    drain(ys.at[0:7], step_recv.at[2])
    total = ys[0].astype(F32)
    for j in range(1, NY):
        total += ys[j].astype(F32)
    psum[...] = total

    own = jnp.where((lane < 64) == even, psum[0], 0.0)
    gram[:, 0:32] = rows_by_rows(own, own, EXACT)
    for s in (1, 2):
        gram[:, 0:32] += rows_by_rows(psum[s], psum[s], EXACT)
    folded = gram[0:8]
    for j in range(1, 4):
        folded += pltpu.roll(gram[8 * j : 8 * j + 8], 32 * j, 1)
    grams[z] = folded
    for to in z_peers:
        remote(grams.at[z], grams.at[z], tail_sent.at[2], tail_recv.at[2], to).start()

    add_b(1, psum[1])
    add_b(2, psum[2])

    @pl.when(par == 0)
    def _():
        add_b(0, psum[0])

    for j in range(NZ):
        bpack[j, 0:32] = bsum[j, :, 0:DEPTH]
        for i in range(4):
            bpack[j, 32:40, 16 * i : 16 * i + 16] = bsum[j, 8 * i : 8 * i + 8, DEPTH:TOK]
    for d in far:
        t = (z + d) % NZ
        remote(bpack.at[t], bs.at[z], tail_sent.at[3], tail_recv.at[3], (dp, t)).start()
    bs[z] = bpack[z]

    drain(grams.at[0:7], tail_recv.at[2])
    folded = grams[0]
    for j in range(1, NZ):
        folded += grams[j]
    line = lax.broadcasted_iota(jnp.int32, (32, DEPTH), 0)
    work = jnp.concatenate([folded] + [pltpu.roll(folded, DEPTH - 32 * j, 1) for j in range(1, 4)], axis=0)
    work = jnp.where(lane < 32, work, jnp.where(lane - 32 == line, 1.0, 0.0))
    for j in range(32):
        pivot = work[j : j + 1, j : j + 1]
        scale = 1.0 / jnp.sqrt(pivot)
        row = work[j : j + 1, :] * scale
        column = jnp.where(line[:, 0:1] > j, work[:, j : j + 1] * scale, 0.0)
        work = jnp.where(line == j, row, work - column * row)
    inverse = pltpu.roll(work, DEPTH - 32, 1)[:, 0:32]

    units = [jnp.dot(inverse, psum[s], preferred_element_type=F32, precision=EXACT) for s in range(3)]
    middle_unit, first_unit, second_unit = [unit * math.sqrt(HD) for unit in units]
    first_turned, second_turned = pltpu.roll(first_unit, 64, 1), pltpu.roll(second_unit, 64, 1)
    low = lane < 64
    middle_turned = pltpu.roll(middle_unit, 64, 1)
    basis[:, 0:128] = jnp.where(even, first_unit, jnp.where(low, middle_turned, first_turned))
    basis[:, 128:256] = jnp.where(even, second_unit, jnp.where(low, first_turned, second_turned))
    basis[:, 256:384] = jnp.where(even, middle_unit, second_turned)

    wide = 640
    units[0] = jnp.where(even, units[0], pltpu.roll(units[0], 64, 1))
    middle_bf, first_bf, second_bf = [unit.astype(BF16) for unit in units]
    for j in range(4):
        cols = slice(wide * j, wide * (j + 1))
        part[:, cols] = (
            jnp.dot(first_bf, er[pl.ds(head_row, DEPTH), cols], preferred_element_type=F32)
            + jnp.dot(second_bf, er[pl.ds(pl.multiple_of(head_row + DEPTH, 64), DEPTH), cols], preferred_element_type=F32)
            + jnp.dot(middle_bf[:, 0:64], er[pl.ds(half_row, 64), cols], preferred_element_type=F32)
        )

    drain(bs.at[0:7], tail_recv.at[3])
    summed = bs[0]
    for j in range(1, NZ):
        summed += bs[j]
    rest = jnp.concatenate([summed[32:40, 16 * i : 16 * i + 16] for i in range(4)], axis=0)
    a_proj = jnp.dot(inverse, summed[0:32], preferred_element_type=F32, precision=EXACT).astype(BF16)
    a_rest = jnp.dot(inverse, rest, preferred_element_type=F32, precision=EXACT).astype(BF16)
    for j in range(4):
        cols = slice(wide * j, wide * (j + 1))
        found = part[:, cols] + jnp.dot(a_proj, og[0:DEPTH, cols], preferred_element_type=F32)
        found += jnp.dot(a_rest, og[DEPTH:TOK, cols], preferred_element_type=F32)
        send[j] = found[0:16].astype(BF16)
        send[4 + j] = found[16:32].astype(BF16)

    for d in far:
        t = (z + d) % NZ
        remote(send.at[t], got.at[z], tail_sent.at[4], tail_recv.at[4], (dp, t)).start()
    got[z] = send[z]
    drain(got.at[0:7], tail_recv.at[4])
    total = got[0].astype(F32)
    for j in range(1, NZ):
        total += got[j].astype(F32)
    cores2[c] = total
    remote(cores2.at[c], cores2.at[c], tail_sent.at[5], tail_recv.at[5], core_peer).start()
    drain(cores2.at[0], tail_recv.at[5])
    xs2[x] = (cores2[0] + cores2[1]).astype(BF16)
    for to in x_peers:
        remote(xs2.at[x], xs2.at[x], tail_sent.at[6], tail_recv.at[6], to).start()
    drain(xs2.at[0:3], tail_recv.at[6])
    total = xs2[0].astype(F32)
    for j in range(1, NX):
        total += xs2[j].astype(F32)
    ys2[y] = total.astype(BF16)
    for to in y_peers:
        remote(ys2.at[y], ys2.at[y], tail_sent.at[7], tail_recv.at[7], to).start()
    drain(ys2.at[0:7], tail_recv.at[7])
    total = ys2[0].astype(F32)
    for j in range(1, NY):
        total += ys2[j].astype(F32)
    q_out[z] = total.astype(BF16)
    for to in z_peers:
        remote(q_out.at[z], q_out.at[z], tail_sent.at[8], tail_recv.at[8], to).start()
    drain(q_out.at[0:7], tail_recv.at[8])
    for s, i in ((1, 2), (2, 0), (2, 1), (2, 2)):
        left(s, i)

    @pl.when(par == 0)
    def _():
        drain(others, step_sent.at[3])

    drain(mem.at[0], step_sent.at[4])
    drain(cores.at[0], step_sent.at[0])
    drain(xs.at[0:3], step_sent.at[1])
    drain(ys.at[0:7], step_sent.at[2])
    drain(frames.at[0:7], tail_sent.at[0])
    drain(dys.at[0:7], tail_sent.at[1])
    drain(grams.at[0:7], tail_sent.at[2])
    drain(bs.at[0:7], tail_sent.at[3])
    drain(got.at[0:7], tail_sent.at[4])
    drain(cores2.at[0], tail_sent.at[5])
    drain(xs2.at[0:3], tail_sent.at[6])
    drain(ys2.at[0:7], tail_sent.at[7])
    drain(q_out.at[0:7], tail_sent.at[8])


def finish(wide_basis, parts, basis, q_out):
    basis[...] = wide_basis[:, 0:ROWS]
    for j in range(NZ):
        r, g = j // 4, j % 4
        q_out[16 * r : 16 * r + 16, 640 * g : 640 * (g + 1)] = parts[j].astype(F32) * (1.0 / 64)


def body(queries, keys, values, frame_ids, out_grad, q_prev, error):
    vmem, dma = pltpu.VMEM, pltpu.SemaphoreType.DMA
    basis, q_factor = pl.pallas_call(
        kernel,
        out_shape=(jax.ShapeDtypeStruct((32, 384), F32), jax.ShapeDtypeStruct((NZ, 16, 640), BF16)),
        in_specs=[pl.BlockSpec(memory_space=pl.ANY)] * 7,
        out_specs=(pl.BlockSpec(memory_space=vmem), pl.BlockSpec(memory_space=vmem)),
        scratch_shapes=[
            vmem((3, 3, SEQ, DEPTH), BF16),
            vmem((2, SEQ, DEPTH), BF16),
            vmem((NZ, 1, TOK), jnp.int32),
            vmem((NZ, 32, TOK), BF16),
            vmem((SEQ, SEQ), BF16),
            vmem((3, SEQ, DEPTH), BF16),
            vmem((TOK, HD), BF16),
            vmem((32, HD), BF16),
            vmem((ROWS, HD), BF16),
            vmem((3, 32, DEPTH), F32),
            vmem((3, 32, DEPTH), F32),
            vmem((2, 3, 32, DEPTH), F32),
            vmem((2, 32, DEPTH), F32),
            vmem((NX, 3, 32, DEPTH), BF16),
            vmem((NY, 3, 32, DEPTH), BF16),
            vmem((32, DEPTH), F32),
            vmem((3, 32, DEPTH), F32),
            vmem((32, DEPTH), F32),
            vmem((NZ, 8, DEPTH), F32),
            vmem((NZ, 32, TOK), F32),
            vmem((NZ, 40, DEPTH), F32),
            vmem((NZ, 40, DEPTH), F32),
            vmem((32, HD), F32),
            vmem((NZ, 16, 640), BF16),
            vmem((NZ, 16, 640), BF16),
            vmem((2, 16, 640), F32),
            vmem((NX, 16, 640), BF16),
            vmem((NY, 16, 640), BF16),
            dma((3,)),
            dma((3, 3)),
            dma((3, 3)),
            dma((6,)),
            dma((6,)),
            dma((9,)),
            dma((9,)),
        ],
        compiler_params=pltpu.CompilerParams(
            collective_id=0, has_side_effects=True, vmem_limit_bytes=56 * 1024 * 1024
        ),
    )(queries[0], keys[0], values[0], frame_ids, out_grad[0], q_prev, error[0])
    return pl.pallas_call(
        finish,
        out_shape=(jax.ShapeDtypeStruct((32, ROWS), F32), jax.ShapeDtypeStruct((32, HD), F32)),
    )(basis, q_factor)


def solution(mesh):
    placed = (
        P("dp", "ctx", None),
        P("dp", "ctx", None),
        P("dp", "ctx", None),
        P("dp", "ctx"),
        P("dp", "ctx", None),
        P(),
        P("dp", "ctx", None),
    )
    return jax.shard_map(
        body, mesh=mesh, in_specs=placed, out_specs=(P(None, "ctx"), P()), check_vma=False
    )
```

```python
import functools
import math

import jax
import jax.numpy as jnp
from jax import lax
from jax.experimental import pallas as pl
from jax.experimental.pallas import tpu as pltpu
from jax.sharding import PartitionSpec as P

MESH = pl.DeviceIdType.MESH
F32, BF16 = jnp.float32, jnp.bfloat16
HD = 2560
TOK = 144
SEQ = 1152
NZ, NX, NY = 8, 4, 8
DEPTH = 128
ROWS = 320
BLOCK = 384
EXACT = lax.Precision.HIGHEST
SCALE = math.log2(math.e) / math.sqrt(DEPTH)
SPANS = ((0, 640), (384, 1024), (768, 1152))


def rows_by_rows(left, right, precision=None):
    return lax.dot_general(
        left, right, (((1,), (1,)), ((), ())), preferred_element_type=F32, precision=precision
    )


def kernel(
    q_in, k_in, v_in, fr_in, og_in, qp_in, er_in,
    basis, q_out,
    qkv, code, frames, dys, packed, probs, attn, og, qp, er, mem, tok,
    others, xs, ys, halves, psum, gram, grams, bpack, bs,
    part, send, got, ys2, zs2,
    in_sem, recv, sent, step_recv, step_sent, tail_recv, tail_sent,
):
    dp, z = lax.axis_index("dp"), lax.axis_index("ctx")
    c, y, x = dp % 2, (dp // 2) % NY, dp // (2 * NY)
    zpar = z % 2
    par = (z + c) % 2
    mate = z + 1 - 2 * zpar
    even = zpar == 0
    far = (4, 3, 5, 2, 6, 1, 7)
    z_peers = [(dp, (z + d) % NZ) for d in far]
    w = 2 * x + c
    w_peers = [(((x + d) % NX) * 2 * NY + 2 * y + t, z) for d in (2, 1, 3) for t in (c, 1 - c)]
    w_peers.append((dp + 1 - 2 * c, z))
    y_peers = [(x * 2 * NY + 2 * ((y + d) % NY) + c, z) for d in far]

    def remote(src, dst, ssem, rsem, to):
        return pltpu.make_async_remote_copy(
            src_ref=src, dst_ref=dst, send_sem=ssem, recv_sem=rsem, device_id=to, device_id_type=MESH
        )

    def drain(ref, sem):
        pltpu.make_async_copy(ref, ref, sem).wait()

    loads = [
        pltpu.make_async_copy(src, dst, in_sem.at[i])
        for i, (src, dst) in enumerate(((og_in, og), (qp_in, qp), (er_in, er)))
    ]
    for load in loads:
        load.start()

    everyone = z_peers + w_peers + y_peers
    barrier = pltpu.get_barrier_semaphore()
    for to in everyone:
        pl.semaphore_signal(barrier, inc=1, device_id=to, device_id_type=MESH)
    pl.semaphore_wait(barrier, len(everyone))

    own_rows = pl.ds(pl.multiple_of(z * TOK, 16), TOK)
    tensors = (k_in, q_in, v_in)

    def columns(slot, t):
        head = 5 * (t // 2) + (2 if slot == 0 else 3 * (t % 2) + slot - 1)
        return pl.ds(pl.multiple_of(head * DEPTH, DEPTH), DEPTH)

    def send_to(slot, i, steps):
        for d in steps:
            t = (z + d) % NZ
            source, target = tensors[i].at[:, columns(slot, t)], qkv.at[slot, i, own_rows]
            if d == 0:
                pltpu.make_async_copy(source, target, recv.at[slot, i]).start()
            else:
                remote(source, target, sent.at[slot, i], recv.at[slot, i], (dp, t)).start()

    def send_head(slot, i):
        if slot > 0:
            send_to(slot, i, far + (0,))
            return

        @pl.when(par == 0)
        def _():
            send_to(0, i, (4, 2, 6, 0))

        @pl.when(par == 1)
        def _():
            send_to(0, i, (3, 5, 1, 7))

    def left(slot, i):
        if slot > 0:
            drain(qkv.at[0, i, 0 : 7 * TOK], sent.at[slot, i])
            return

        @pl.when(par == 0)
        def _():
            drain(qkv.at[0, i, 0 : 3 * TOK], sent.at[0, i])

        @pl.when(par == 1)
        def _():
            drain(qkv.at[0, i, 0 : 4 * TOK], sent.at[0, i])

    send_head(0, 0)
    pltpu.make_async_copy(fr_in, frames.at[z], step_recv.at[5]).start()
    for to in z_peers:
        remote(fr_in, frames.at[z], tail_sent.at[0], step_recv.at[5], to).start()
    send_head(0, 1)
    send_head(0, 2)

    loads[0].wait()
    loads[1].wait()
    found = rows_by_rows(qp[...], og[...])
    packed[...] = jnp.zeros_like(packed)
    packed[0:32] = found[:, 0:DEPTH]
    packed[32:48, 0:16] = found[0:16, DEPTH:]
    packed[32:48, 16:32] = found[16:32, DEPTH:]
    dys[z] = packed[...].astype(BF16)
    for to in z_peers:
        remote(dys.at[z], dys.at[z], tail_sent.at[1], tail_recv.at[1], to).start()
    send_head(1, 0)

    loads[2].wait()
    head_row = pl.multiple_of(64 * zpar, 64)
    half_row = pl.multiple_of(256 * (1 - zpar), 64)
    halves[...] = jnp.zeros((32, DEPTH), F32)
    halves[:, 0:64] = rows_by_rows(qp[...], er[pl.ds(half_row, 64), :])
    mine = halves[...]
    mem[0] = jnp.where(even, mine, pltpu.roll(mine, 64, 1))
    remote(mem.at[0], others.at[0], step_sent.at[4], step_recv.at[4], (dp, mate)).start()
    for s in (1, 2):
        rows = pl.ds(pl.multiple_of(head_row + DEPTH * (s - 1), 64), DEPTH)
        mem[s] = rows_by_rows(qp[...], er[rows, :])
    tok[...] = jnp.zeros_like(tok)
    bpack[...] = jnp.zeros_like(bpack)
    gram[...] = jnp.zeros_like(gram)

    drain(frames, step_recv.at[5])
    number = lax.broadcasted_iota(jnp.int32, (16, TOK), 0)
    place = (
        lax.broadcasted_iota(jnp.int32, (16, DEPTH), 0) == lax.broadcasted_iota(jnp.int32, (16, DEPTH), 1)
    ).astype(F32)
    for j in range(NZ):
        row = jnp.broadcast_to(frames[j], (16, TOK))
        for i, value in enumerate((jnp.where(row == number, 1.0, 0.0), jnp.where(row > number, -1e30, 0.0))):
            code[i, j * TOK : (j + 1) * TOK, :] = lax.dot_general(
                value, place, (((0,), (0,)), ((), ())), preferred_element_type=F32
            ).astype(BF16)
    drain(dys.at[0:7], tail_recv.at[1])

    lane = lax.broadcasted_iota(jnp.int32, (32, DEPTH), 1)

    def attend(s):
        drain(qkv.at[s, 0], recv.at[s, 0])
        drain(qkv.at[s, 1], recv.at[s, 1])
        for first, reach in SPANS:
            queries = jnp.concatenate([qkv[s, 1, first : first + BLOCK, :], code[0, first : first + BLOCK, :]], axis=1)
            keys = jnp.concatenate([qkv[s, 0, 0:reach, :], code[1, 0:reach, :]], axis=1)
            scores = rows_by_rows(queries, keys)
            top = jnp.max(scores, axis=1, keepdims=True)
            probs[first : first + BLOCK, 0:reach] = jnp.exp2((scores - top) * SCALE).astype(BF16)
        drain(qkv.at[s, 2], recv.at[s, 2])
        for first, reach in SPANS:
            values = jnp.concatenate([qkv[s, 2, 0:reach, :], jnp.ones((reach, DEPTH), BF16)], axis=1)
            mixed = jnp.dot(probs[first : first + BLOCK, 0:reach], values, preferred_element_type=F32)
            attn[s, first : first + BLOCK, :] = (mixed[:, 0:DEPTH] / mixed[:, DEPTH:]).astype(BF16)
        total = jnp.zeros((32, DEPTH), F32)
        for j in range(NZ):
            main, rest = dys[j, 0:32, :], dys[j, 32:48, :].astype(F32)
            rest = jnp.concatenate([rest, pltpu.roll(rest, DEPTH - 16, 1)], axis=0)[:, 0:16].astype(BF16)
            total += jnp.dot(main, attn[s, j * TOK : j * TOK + DEPTH, :], preferred_element_type=F32)
            total += jnp.dot(rest, attn[s, j * TOK + DEPTH : (j + 1) * TOK, :], preferred_element_type=F32)
        tok[s] = total

    def head(s, carry):
        @pl.when(s == 0)
        def _():
            for i, ahead in enumerate(((1, 1), (1, 2), (2, 0))):
                left(0, i)
                send_head(*ahead)

        @pl.when(s == 1)
        def _():
            for i, ahead in enumerate(((2, 1), (2, 2))):
                left(1, i)
                send_head(*ahead)

        @pl.when(jnp.logical_or(s > 0, par == 0))
        def _():
            attend(s)

        @pl.when(jnp.logical_and(s == 0, par == 0))
        def _():
            remote(tok.at[0], others.at[1], step_sent.at[3], step_recv.at[3], (dp, mate)).start()

        return carry

    lax.fori_loop(0, 3, head, 0)

    drain(others.at[0], step_recv.at[4])

    @pl.when(par == 1)
    def _():
        attn[0] = jnp.zeros((SEQ, DEPTH), BF16)
        drain(others.at[1], step_recv.at[3])
        tok[0] = others[1]

    xs[w, 0] = ((mem[0] + others[0]) + tok[0]).astype(BF16)
    xs[w, 1] = (mem[1] + tok[1]).astype(BF16)
    xs[w, 2] = (mem[2] + tok[2]).astype(BF16)
    for to in w_peers:
        remote(xs.at[w], xs.at[w], step_sent.at[1], step_recv.at[1], to).start()
    drain(xs.at[0:7], step_recv.at[1])
    total = xs[0].astype(F32)
    for j in range(1, 8):
        total += xs[j].astype(F32)
    ys[y] = total.astype(BF16)
    for to in y_peers:
        remote(ys.at[y], ys.at[y], step_sent.at[2], step_recv.at[2], to).start()
    drain(ys.at[0:7], step_recv.at[2])
    total = ys[0].astype(F32)
    for j in range(1, NY):
        total += ys[j].astype(F32)
    psum[...] = total

    own = jnp.where((lane < 64) == even, psum[0], 0.0)
    gram[:, 0:32] = rows_by_rows(own, own, EXACT)
    for s in (1, 2):
        gram[:, 0:32] += rows_by_rows(psum[s], psum[s], EXACT)
    folded = gram[0:8]
    for j in range(1, 4):
        folded += pltpu.roll(gram[8 * j : 8 * j + 8], 32 * j, 1)
    grams[z] = folded
    for to in z_peers:
        remote(grams.at[z], grams.at[z], tail_sent.at[2], tail_recv.at[2], to).start()

    rows = jnp.concatenate([psum[0], psum[1], psum[2]], axis=1)
    high = rows.astype(BF16)
    both = jnp.concatenate([high, (rows - high.astype(F32)).astype(BF16)], axis=0)
    for d in far + (0,):
        t = (z + d) % NZ
        first = pl.multiple_of(t * TOK, 16)
        for count, start in ((DEPTH, 0), (TOK - DEPTH, DEPTH)):
            heads = [attn[s, pl.ds(first + start, count), :] for s in range(3)]
            found = rows_by_rows(both, jnp.concatenate(heads, axis=1))
            found = found[0:32] + found[32:64]
            if start == 0:
                bpack[t, 0:32] = found
            else:
                for i in range(4):
                    bpack[t, 32:40, 16 * i : 16 * i + 16] = found[8 * i : 8 * i + 8]
        if d > 0:
            remote(bpack.at[t], bs.at[z], tail_sent.at[3], tail_recv.at[3], (dp, t)).start()
        else:
            bs[z] = bpack[z]

    drain(grams.at[0:7], tail_recv.at[2])
    folded = grams[0]
    for j in range(1, NZ):
        folded += grams[j]
    line = lax.broadcasted_iota(jnp.int32, (32, DEPTH), 0)
    work = jnp.concatenate([folded] + [pltpu.roll(folded, DEPTH - 32 * j, 1) for j in range(1, 4)], axis=0)
    work = jnp.where(lane < 32, work, jnp.where(lane - 32 == line, 1.0, 0.0))
    for j in range(32):
        pivot = work[j : j + 1, j : j + 1]
        scale = lax.rsqrt(pivot)
        row = work[j : j + 1, :] * scale
        column = jnp.where(line[:, 0:1] > j, work[:, j : j + 1] * scale, 0.0)
        work = jnp.where(line == j, row, work - column * row)
    inverse = pltpu.roll(work, DEPTH - 32, 1)[:, 0:32]

    units = [jnp.dot(inverse, psum[s], preferred_element_type=F32, precision=EXACT) for s in range(3)]
    middle_unit, first_unit, second_unit = [unit * math.sqrt(HD) for unit in units]
    first_turned, second_turned = pltpu.roll(first_unit, 64, 1), pltpu.roll(second_unit, 64, 1)
    low = lane < 64
    middle_turned = pltpu.roll(middle_unit, 64, 1)
    basis[:, 0:128] = jnp.where(even, first_unit, jnp.where(low, middle_turned, first_turned))
    basis[:, 128:256] = jnp.where(even, second_unit, jnp.where(low, first_turned, second_turned))
    basis[:, 256:384] = jnp.where(even, middle_unit, second_turned)

    wide = 640
    units[0] = jnp.where(even, units[0], pltpu.roll(units[0], 64, 1))
    middle_bf, first_bf, second_bf = [unit.astype(BF16) for unit in units]
    for j in range(4):
        cols = slice(wide * j, wide * (j + 1))
        part[:, cols] = (
            jnp.dot(first_bf, er[pl.ds(head_row, DEPTH), cols], preferred_element_type=F32)
            + jnp.dot(second_bf, er[pl.ds(pl.multiple_of(head_row + DEPTH, 64), DEPTH), cols], preferred_element_type=F32)
            + jnp.dot(middle_bf[:, 0:64], er[pl.ds(half_row, 64), cols], preferred_element_type=F32)
        )

    drain(bs.at[0:7], tail_recv.at[3])
    summed = bs[0]
    for j in range(1, NZ):
        summed += bs[j]
    rest = jnp.concatenate([summed[32:40, 16 * i : 16 * i + 16] for i in range(4)], axis=0)
    a_proj = jnp.dot(inverse, summed[0:32], preferred_element_type=F32, precision=EXACT).astype(BF16)
    a_rest = jnp.dot(inverse, rest, preferred_element_type=F32, precision=EXACT).astype(BF16)
    for j in range(4):
        cols = slice(wide * j, wide * (j + 1))
        found = part[:, cols] + jnp.dot(a_proj, og[0:DEPTH, cols], preferred_element_type=F32)
        found += jnp.dot(a_rest, og[DEPTH:TOK, cols], preferred_element_type=F32)
        for r in range(2):
            place = 4 * r + j
            send[place] = found[16 * r : 16 * r + 16].astype(BF16)

            @pl.when(w == place)
            def _():
                got[place] = send[place]

            @pl.when(w != place)
            def _():
                to = ((place // 2) * 2 * NY + 2 * y + place % 2, z)
                remote(send.at[place], got.at[w], tail_sent.at[4], tail_recv.at[4], to).start()

    def summed_over(blocks):
        total = blocks[0].astype(F32)
        for j in range(1, 8):
            total += blocks[j].astype(F32)
        return total.astype(BF16)

    drain(got.at[0:7], tail_recv.at[4])
    ys2[y] = summed_over(got)
    for to in y_peers:
        remote(ys2.at[y], ys2.at[y], tail_sent.at[7], tail_recv.at[7], to).start()
    drain(ys2.at[0:7], tail_recv.at[7])
    zs2[z] = summed_over(ys2)
    for to in z_peers:
        remote(zs2.at[z], zs2.at[z], tail_sent.at[6], tail_recv.at[6], to).start()
    drain(zs2.at[0:7], tail_recv.at[6])
    q_out[w] = summed_over(zs2)
    for to in w_peers:
        remote(q_out.at[w], q_out.at[w], tail_sent.at[8], tail_recv.at[8], to).start()
    drain(q_out.at[0:7], tail_recv.at[8])

    for s, i in ((1, 2), (2, 0), (2, 1), (2, 2)):
        left(s, i)

    @pl.when(par == 0)
    def _():
        drain(others.at[1], step_sent.at[3])

    drain(mem.at[0], step_sent.at[4])
    drain(xs.at[0:7], step_sent.at[1])
    drain(ys.at[0:7], step_sent.at[2])
    drain(frames.at[0:7], tail_sent.at[0])
    drain(dys.at[0:7], tail_sent.at[1])
    drain(grams.at[0:7], tail_sent.at[2])
    drain(bs.at[0:7], tail_sent.at[3])
    drain(got.at[0:7], tail_sent.at[4])
    drain(zs2.at[0:7], tail_sent.at[6])
    drain(ys2.at[0:7], tail_sent.at[7])
    drain(q_out.at[0:7], tail_sent.at[8])


def finish(wide_basis, parts, basis, q_out):
    basis[...] = wide_basis[:, 0:ROWS]
    for j in range(NZ):
        r, g = j // 4, j % 4
        q_out[16 * r : 16 * r + 16, 640 * g : 640 * (g + 1)] = parts[j].astype(F32) * (1.0 / 64)


def body(queries, keys, values, frame_ids, out_grad, q_prev, error):
    vmem, dma = pltpu.VMEM, pltpu.SemaphoreType.DMA
    basis, q_factor = pl.pallas_call(
        kernel,
        out_shape=(jax.ShapeDtypeStruct((32, 384), F32), jax.ShapeDtypeStruct((NZ, 16, 640), BF16)),
        in_specs=[pl.BlockSpec(memory_space=pl.ANY)] * 7,
        out_specs=(pl.BlockSpec(memory_space=vmem), pl.BlockSpec(memory_space=vmem)),
        scratch_shapes=[
            vmem((3, 3, SEQ, DEPTH), BF16),
            vmem((2, SEQ, DEPTH), BF16),
            vmem((NZ, 1, TOK), jnp.int32),
            vmem((NZ, 48, DEPTH), BF16),
            vmem((48, DEPTH), F32),
            vmem((SEQ, SEQ), BF16),
            vmem((3, SEQ, DEPTH), BF16),
            vmem((TOK, HD), BF16),
            vmem((32, HD), BF16),
            vmem((ROWS, HD), BF16),
            vmem((3, 32, DEPTH), F32),
            vmem((3, 32, DEPTH), F32),
            vmem((2, 32, DEPTH), F32),
            vmem((8, 3, 32, DEPTH), BF16),
            vmem((NY, 3, 32, DEPTH), BF16),
            vmem((32, DEPTH), F32),
            vmem((3, 32, DEPTH), F32),
            vmem((32, DEPTH), F32),
            vmem((NZ, 8, DEPTH), F32),
            vmem((NZ, 40, DEPTH), F32),
            vmem((NZ, 40, DEPTH), F32),
            vmem((32, HD), F32),
            vmem((NZ, 16, 640), BF16),
            vmem((NZ, 16, 640), BF16),
            vmem((NY, 16, 640), BF16),
            vmem((NZ, 16, 640), BF16),
            dma((3,)),
            dma((3, 3)),
            dma((3, 3)),
            dma((6,)),
            dma((6,)),
            dma((9,)),
            dma((9,)),
        ],
        compiler_params=pltpu.CompilerParams(
            collective_id=0, has_side_effects=True, vmem_limit_bytes=56 * 1024 * 1024
        ),
    )(queries[0], keys[0], values[0], frame_ids, out_grad[0], q_prev, error[0])
    return pl.pallas_call(
        finish,
        out_shape=(jax.ShapeDtypeStruct((32, ROWS), F32), jax.ShapeDtypeStruct((32, HD), F32)),
    )(basis, q_factor)


def solution(mesh):
    placed = (
        P("dp", "ctx", None),
        P("dp", "ctx", None),
        P("dp", "ctx", None),
        P("dp", "ctx"),
        P("dp", "ctx", None),
        P(),
        P("dp", "ctx", None),
    )
    return jax.shard_map(
        body, mesh=mesh, in_specs=placed, out_specs=(P(None, "ctx"), P()), check_vma=False
    )
```

```python
import functools
import math

import jax
import jax.numpy as jnp
from jax import lax
from jax.experimental import pallas as pl
from jax.experimental.pallas import tpu as pltpu
from jax.sharding import PartitionSpec as P

MESH = pl.DeviceIdType.MESH
F32, BF16 = jnp.float32, jnp.bfloat16
HD = 2560
TOK = 144
SEQ = 1152
NZ, NX, NY = 8, 4, 8
DEPTH = 128
ROWS = 320
BLOCK = 384
EXACT = lax.Precision.HIGHEST
SCALE = math.log2(math.e) / math.sqrt(DEPTH)
SPANS = ((0, 640), (384, 1024), (768, 1152))


def rows_by_rows(left, right, precision=None):
    return lax.dot_general(
        left, right, (((1,), (1,)), ((), ())), preferred_element_type=F32, precision=precision
    )


def kernel(
    q_in, k_in, v_in, fr_in, og_in, qp_in, er_in,
    basis, q_out,
    qkv, code, frames, dys, packed, probs, attn, og, qp, er, mem, tok,
    others, xs, ys, xs1, ys1, halves, psum, gram, grams, bpack, bs,
    part, send, got, ys2, zs2,
    in_sem, recv, sent, step_recv, step_sent, tail_recv, tail_sent,
):
    dp, z = lax.axis_index("dp"), lax.axis_index("ctx")
    c, y, x = dp % 2, (dp // 2) % NY, dp // (2 * NY)
    zpar = z % 2
    par = (z + c) % 2
    mate = z + 1 - 2 * zpar
    even = zpar == 0
    far = (4, 3, 5, 2, 6, 1, 7)
    z_peers = [(dp, (z + d) % NZ) for d in far]
    w = 2 * x + c
    w_peers = [(((x + d) % NX) * 2 * NY + 2 * y + t, z) for d in (2, 1, 3) for t in (c, 1 - c)]
    w_peers.append((dp + 1 - 2 * c, z))
    y_peers = [(x * 2 * NY + 2 * ((y + d) % NY) + c, z) for d in far]

    def remote(src, dst, ssem, rsem, to):
        return pltpu.make_async_remote_copy(
            src_ref=src, dst_ref=dst, send_sem=ssem, recv_sem=rsem, device_id=to, device_id_type=MESH
        )

    def drain(ref, sem):
        pltpu.make_async_copy(ref, ref, sem).wait()

    loads = [
        pltpu.make_async_copy(src, dst, in_sem.at[i])
        for i, (src, dst) in enumerate(((og_in, og), (qp_in, qp), (er_in, er)))
    ]
    for load in loads:
        load.start()

    everyone = z_peers + w_peers + y_peers
    barrier = pltpu.get_barrier_semaphore()
    for to in everyone:
        pl.semaphore_signal(barrier, inc=1, device_id=to, device_id_type=MESH)
    pl.semaphore_wait(barrier, len(everyone))

    own_rows = pl.ds(pl.multiple_of(z * TOK, 16), TOK)
    tensors = (k_in, q_in, v_in)

    def columns(slot, t):
        head = 5 * (t // 2) + (2 if slot == 0 else 3 * (t % 2) + slot - 1)
        return pl.ds(pl.multiple_of(head * DEPTH, DEPTH), DEPTH)

    def send_to(slot, i, steps):
        for d in steps:
            t = (z + d) % NZ
            source, target = tensors[i].at[:, columns(slot, t)], qkv.at[slot, i, own_rows]
            if d == 0:
                pltpu.make_async_copy(source, target, recv.at[slot, i]).start()
            else:
                remote(source, target, sent.at[slot, i], recv.at[slot, i], (dp, t)).start()

    def send_head(slot, i):
        if slot > 0:
            send_to(slot, i, far + (0,))
            return

        @pl.when(par == 0)
        def _():
            send_to(0, i, (4, 2, 6, 0))

        @pl.when(par == 1)
        def _():
            send_to(0, i, (3, 5, 1, 7))

    def left(slot, i):
        if slot > 0:
            drain(qkv.at[0, i, 0 : 7 * TOK], sent.at[slot, i])
            return

        @pl.when(par == 0)
        def _():
            drain(qkv.at[0, i, 0 : 3 * TOK], sent.at[0, i])

        @pl.when(par == 1)
        def _():
            drain(qkv.at[0, i, 0 : 4 * TOK], sent.at[0, i])

    send_head(0, 0)
    pltpu.make_async_copy(fr_in, frames.at[z], step_recv.at[5]).start()
    for to in z_peers:
        remote(fr_in, frames.at[z], tail_sent.at[0], step_recv.at[5], to).start()
    send_head(0, 1)
    send_head(0, 2)

    loads[0].wait()
    loads[1].wait()
    found = rows_by_rows(qp[...], og[...])
    packed[...] = jnp.zeros_like(packed)
    packed[0:32] = found[:, 0:DEPTH]
    packed[32:48, 0:16] = found[0:16, DEPTH:]
    packed[32:48, 16:32] = found[16:32, DEPTH:]
    dys[z] = packed[...].astype(BF16)
    for to in z_peers:
        remote(dys.at[z], dys.at[z], tail_sent.at[1], tail_recv.at[1], to).start()
    send_head(1, 0)

    loads[2].wait()
    head_row = pl.multiple_of(64 * zpar, 64)
    half_row = pl.multiple_of(256 * (1 - zpar), 64)
    halves[...] = jnp.zeros((32, DEPTH), F32)
    halves[:, 0:64] = rows_by_rows(qp[...], er[pl.ds(half_row, 64), :])
    mine = halves[...]
    mem[0] = jnp.where(even, mine, pltpu.roll(mine, 64, 1))
    remote(mem.at[0], others.at[0], step_sent.at[4], step_recv.at[4], (dp, mate)).start()
    for s in (1, 2):
        rows = pl.ds(pl.multiple_of(head_row + DEPTH * (s - 1), 64), DEPTH)
        mem[s] = rows_by_rows(qp[...], er[rows, :])
    tok[...] = jnp.zeros_like(tok)
    bpack[...] = jnp.zeros_like(bpack)
    gram[...] = jnp.zeros_like(gram)

    drain(frames, step_recv.at[5])
    number = lax.broadcasted_iota(jnp.int32, (16, TOK), 0)
    place = (
        lax.broadcasted_iota(jnp.int32, (16, DEPTH), 0) == lax.broadcasted_iota(jnp.int32, (16, DEPTH), 1)
    ).astype(F32)
    for j in range(NZ):
        row = jnp.broadcast_to(frames[j], (16, TOK))
        for i, value in enumerate((jnp.where(row == number, 1.0, 0.0), jnp.where(row > number, -1e30, 0.0))):
            code[i, j * TOK : (j + 1) * TOK, :] = lax.dot_general(
                value, place, (((0,), (0,)), ((), ())), preferred_element_type=F32
            ).astype(BF16)
    drain(dys.at[0:7], tail_recv.at[1])

    lane = lax.broadcasted_iota(jnp.int32, (32, DEPTH), 1)

    def attend(s):
        drain(qkv.at[s, 0], recv.at[s, 0])
        drain(qkv.at[s, 1], recv.at[s, 1])
        for first, reach in SPANS:
            queries = jnp.concatenate([qkv[s, 1, first : first + BLOCK, :], code[0, first : first + BLOCK, :]], axis=1)
            keys = jnp.concatenate([qkv[s, 0, 0:reach, :], code[1, 0:reach, :]], axis=1)
            scores = rows_by_rows(queries, keys)
            top = jnp.max(scores, axis=1, keepdims=True)
            probs[first : first + BLOCK, 0:reach] = jnp.exp2((scores - top) * SCALE).astype(BF16)
        drain(qkv.at[s, 2], recv.at[s, 2])
        for first, reach in SPANS:
            values = jnp.concatenate([qkv[s, 2, 0:reach, :], jnp.ones((reach, DEPTH), BF16)], axis=1)
            mixed = jnp.dot(probs[first : first + BLOCK, 0:reach], values, preferred_element_type=F32)
            attn[s, first : first + BLOCK, :] = (mixed[:, 0:DEPTH] / mixed[:, DEPTH:]).astype(BF16)
        total = jnp.zeros((32, DEPTH), F32)
        for j in range(NZ):
            main, rest = dys[j, 0:32, :], dys[j, 32:48, :].astype(F32)
            rest = jnp.concatenate([rest, pltpu.roll(rest, DEPTH - 16, 1)], axis=0)[:, 0:16].astype(BF16)
            total += jnp.dot(main, attn[s, j * TOK : j * TOK + DEPTH, :], preferred_element_type=F32)
            total += jnp.dot(rest, attn[s, j * TOK + DEPTH : (j + 1) * TOK, :], preferred_element_type=F32)
        tok[s] = total

    def over(blocks):
        total = blocks[0].astype(F32)
        for j in range(1, 8):
            total += blocks[j].astype(F32)
        return total

    def head(s, carry):
        @pl.when(s == 0)
        def _():
            for i, ahead in enumerate(((1, 1), (1, 2), (2, 0))):
                left(0, i)
                send_head(*ahead)

        @pl.when(s == 1)
        def _():
            left(1, 0)
            send_head(2, 1)

        @pl.when(jnp.logical_or(s > 0, par == 0))
        def _():
            attend(s)

        @pl.when(jnp.logical_and(s == 0, par == 0))
        def _():
            remote(tok.at[0], others.at[1], step_sent.at[3], step_recv.at[3], (dp, mate)).start()

        @pl.when(s == 1)
        def _():
            drain(others.at[0], step_recv.at[4])

            @pl.when(par == 1)
            def _():
                attn[0] = jnp.zeros((SEQ, DEPTH), BF16)
                drain(others.at[1], step_recv.at[3])
                tok[0] = others[1]

            xs[w, 0] = ((mem[0] + others[0]) + tok[0]).astype(BF16)
            xs[w, 1] = (mem[1] + tok[1]).astype(BF16)
            for to in w_peers:
                remote(xs.at[w], xs.at[w], step_sent.at[1], step_recv.at[1], to).start()
            left(1, 1)
            send_head(2, 2)
            drain(xs.at[0:7], step_recv.at[1])
            ys[y] = over(xs).astype(BF16)
            for to in y_peers:
                remote(ys.at[y], ys.at[y], step_sent.at[2], step_recv.at[2], to).start()

        return carry

    lax.fori_loop(0, 3, head, 0)

    xs1[w] = (mem[2] + tok[2]).astype(BF16)
    for to in w_peers:
        remote(xs1.at[w], xs1.at[w], tail_sent.at[5], tail_recv.at[5], to).start()
    drain(ys.at[0:7], step_recv.at[2])
    psum[0:2] = over(ys)
    drain(xs1.at[0:7], tail_recv.at[5])
    ys1[y] = over(xs1).astype(BF16)
    for to in y_peers:
        remote(ys1.at[y], ys1.at[y], step_sent.at[0], step_recv.at[0], to).start()
    drain(ys1.at[0:7], step_recv.at[0])
    psum[2] = over(ys1)

    own = jnp.where((lane < 64) == even, psum[0], 0.0)
    gram[:, 0:32] = rows_by_rows(own, own, EXACT)
    for s in (1, 2):
        gram[:, 0:32] += rows_by_rows(psum[s], psum[s], EXACT)
    folded = gram[0:8]
    for j in range(1, 4):
        folded += pltpu.roll(gram[8 * j : 8 * j + 8], 32 * j, 1)
    grams[z] = folded
    for to in z_peers:
        remote(grams.at[z], grams.at[z], tail_sent.at[2], tail_recv.at[2], to).start()

    rows = jnp.concatenate([psum[0], psum[1], psum[2]], axis=1)
    high = rows.astype(BF16)
    both = jnp.concatenate([high, (rows - high.astype(F32)).astype(BF16)], axis=0)
    for d in far + (0,):
        t = (z + d) % NZ
        first = pl.multiple_of(t * TOK, 16)
        for count, start in ((DEPTH, 0), (TOK - DEPTH, DEPTH)):
            heads = [attn[s, pl.ds(first + start, count), :] for s in range(3)]
            found = rows_by_rows(both, jnp.concatenate(heads, axis=1))
            found = found[0:32] + found[32:64]
            if start == 0:
                bpack[t, 0:32] = found
            else:
                for i in range(4):
                    bpack[t, 32:40, 16 * i : 16 * i + 16] = found[8 * i : 8 * i + 8]
        if d > 0:
            remote(bpack.at[t], bs.at[z], tail_sent.at[3], tail_recv.at[3], (dp, t)).start()
        else:
            bs[z] = bpack[z]

    drain(grams.at[0:7], tail_recv.at[2])
    folded = grams[0]
    for j in range(1, NZ):
        folded += grams[j]
    line = lax.broadcasted_iota(jnp.int32, (32, DEPTH), 0)
    work = jnp.concatenate([folded] + [pltpu.roll(folded, DEPTH - 32 * j, 1) for j in range(1, 4)], axis=0)
    work = jnp.where(lane < 32, work, jnp.where(lane - 32 == line, 1.0, 0.0))
    for j in range(32):
        pivot = work[j : j + 1, j : j + 1]
        scale = lax.rsqrt(pivot)
        row = work[j : j + 1, :] * scale
        column = jnp.where(line[:, 0:1] > j, work[:, j : j + 1] * scale, 0.0)
        work = jnp.where(line == j, row, work - column * row)
    inverse = pltpu.roll(work, DEPTH - 32, 1)[:, 0:32]

    units = [jnp.dot(inverse, psum[s], preferred_element_type=F32, precision=EXACT) for s in range(3)]
    middle_unit, first_unit, second_unit = [unit * math.sqrt(HD) for unit in units]
    first_turned, second_turned = pltpu.roll(first_unit, 64, 1), pltpu.roll(second_unit, 64, 1)
    low = lane < 64
    middle_turned = pltpu.roll(middle_unit, 64, 1)
    basis[:, 0:128] = jnp.where(even, first_unit, jnp.where(low, middle_turned, first_turned))
    basis[:, 128:256] = jnp.where(even, second_unit, jnp.where(low, first_turned, second_turned))
    basis[:, 256:384] = jnp.where(even, middle_unit, second_turned)

    wide = 640
    units[0] = jnp.where(even, units[0], pltpu.roll(units[0], 64, 1))
    middle_bf, first_bf, second_bf = [unit.astype(BF16) for unit in units]
    for j in range(4):
        cols = slice(wide * j, wide * (j + 1))
        part[:, cols] = (
            jnp.dot(first_bf, er[pl.ds(head_row, DEPTH), cols], preferred_element_type=F32)
            + jnp.dot(second_bf, er[pl.ds(pl.multiple_of(head_row + DEPTH, 64), DEPTH), cols], preferred_element_type=F32)
            + jnp.dot(middle_bf[:, 0:64], er[pl.ds(half_row, 64), cols], preferred_element_type=F32)
        )

    drain(bs.at[0:7], tail_recv.at[3])
    summed = bs[0]
    for j in range(1, NZ):
        summed += bs[j]
    rest = jnp.concatenate([summed[32:40, 16 * i : 16 * i + 16] for i in range(4)], axis=0)
    a_proj = jnp.dot(inverse, summed[0:32], preferred_element_type=F32, precision=EXACT).astype(BF16)
    a_rest = jnp.dot(inverse, rest, preferred_element_type=F32, precision=EXACT).astype(BF16)
    for j in range(4):
        cols = slice(wide * j, wide * (j + 1))
        found = part[:, cols] + jnp.dot(a_proj, og[0:DEPTH, cols], preferred_element_type=F32)
        found += jnp.dot(a_rest, og[DEPTH:TOK, cols], preferred_element_type=F32)
        for r in range(2):
            place = 4 * r + j
            send[place] = found[16 * r : 16 * r + 16].astype(BF16)

            @pl.when(w == place)
            def _():
                got[place] = send[place]

            @pl.when(w != place)
            def _():
                to = ((place // 2) * 2 * NY + 2 * y + place % 2, z)
                remote(send.at[place], got.at[w], tail_sent.at[4], tail_recv.at[4], to).start()

    drain(got.at[0:7], tail_recv.at[4])
    ys2[y] = over(got).astype(BF16)
    for to in y_peers:
        remote(ys2.at[y], ys2.at[y], tail_sent.at[7], tail_recv.at[7], to).start()
    drain(ys2.at[0:7], tail_recv.at[7])
    zs2[z] = over(ys2).astype(BF16)
    for to in z_peers:
        remote(zs2.at[z], zs2.at[z], tail_sent.at[6], tail_recv.at[6], to).start()
    drain(zs2.at[0:7], tail_recv.at[6])
    q_out[w] = over(zs2).astype(BF16)
    for to in w_peers:
        remote(q_out.at[w], q_out.at[w], tail_sent.at[8], tail_recv.at[8], to).start()
    drain(q_out.at[0:7], tail_recv.at[8])

    for s, i in ((1, 2), (2, 0), (2, 1), (2, 2)):
        left(s, i)

    @pl.when(par == 0)
    def _():
        drain(others.at[1], step_sent.at[3])

    drain(mem.at[0], step_sent.at[4])
    drain(xs1.at[0:7], tail_sent.at[5])
    drain(ys1.at[0:7], step_sent.at[0])
    drain(xs.at[0:7], step_sent.at[1])
    drain(ys.at[0:7], step_sent.at[2])
    drain(frames.at[0:7], tail_sent.at[0])
    drain(dys.at[0:7], tail_sent.at[1])
    drain(grams.at[0:7], tail_sent.at[2])
    drain(bs.at[0:7], tail_sent.at[3])
    drain(got.at[0:7], tail_sent.at[4])
    drain(zs2.at[0:7], tail_sent.at[6])
    drain(ys2.at[0:7], tail_sent.at[7])
    drain(q_out.at[0:7], tail_sent.at[8])


def finish(wide_basis, parts, basis, q_out):
    basis[...] = wide_basis[:, 0:ROWS]
    for j in range(NZ):
        r, g = j // 4, j % 4
        q_out[16 * r : 16 * r + 16, 640 * g : 640 * (g + 1)] = parts[j].astype(F32) * (1.0 / 64)


def body(queries, keys, values, frame_ids, out_grad, q_prev, error):
    vmem, dma = pltpu.VMEM, pltpu.SemaphoreType.DMA
    basis, q_factor = pl.pallas_call(
        kernel,
        out_shape=(jax.ShapeDtypeStruct((32, 384), F32), jax.ShapeDtypeStruct((NZ, 16, 640), BF16)),
        in_specs=[pl.BlockSpec(memory_space=pl.ANY)] * 7,
        out_specs=(pl.BlockSpec(memory_space=vmem), pl.BlockSpec(memory_space=vmem)),
        scratch_shapes=[
            vmem((3, 3, SEQ, DEPTH), BF16),
            vmem((2, SEQ, DEPTH), BF16),
            vmem((NZ, 1, TOK), jnp.int32),
            vmem((NZ, 48, DEPTH), BF16),
            vmem((48, DEPTH), F32),
            vmem((SEQ, SEQ), BF16),
            vmem((3, SEQ, DEPTH), BF16),
            vmem((TOK, HD), BF16),
            vmem((32, HD), BF16),
            vmem((ROWS, HD), BF16),
            vmem((3, 32, DEPTH), F32),
            vmem((3, 32, DEPTH), F32),
            vmem((2, 32, DEPTH), F32),
            vmem((8, 2, 32, DEPTH), BF16),
            vmem((NY, 2, 32, DEPTH), BF16),
            vmem((8, 32, DEPTH), BF16),
            vmem((NY, 32, DEPTH), BF16),
            vmem((32, DEPTH), F32),
            vmem((3, 32, DEPTH), F32),
            vmem((32, DEPTH), F32),
            vmem((NZ, 8, DEPTH), F32),
            vmem((NZ, 40, DEPTH), F32),
            vmem((NZ, 40, DEPTH), F32),
            vmem((32, HD), F32),
            vmem((NZ, 16, 640), BF16),
            vmem((NZ, 16, 640), BF16),
            vmem((NY, 16, 640), BF16),
            vmem((NZ, 16, 640), BF16),
            dma((3,)),
            dma((3, 3)),
            dma((3, 3)),
            dma((6,)),
            dma((6,)),
            dma((9,)),
            dma((9,)),
        ],
        compiler_params=pltpu.CompilerParams(
            collective_id=0, has_side_effects=True, vmem_limit_bytes=56 * 1024 * 1024
        ),
    )(queries[0], keys[0], values[0], frame_ids, out_grad[0], q_prev, error[0])
    return pl.pallas_call(
        finish,
        out_shape=(jax.ShapeDtypeStruct((32, ROWS), F32), jax.ShapeDtypeStruct((32, HD), F32)),
    )(basis, q_factor)


def solution(mesh):
    placed = (
        P("dp", "ctx", None),
        P("dp", "ctx", None),
        P("dp", "ctx", None),
        P("dp", "ctx"),
        P("dp", "ctx", None),
        P(),
        P("dp", "ctx", None),
    )
    return jax.shard_map(
        body, mesh=mesh, in_specs=placed, out_specs=(P(None, "ctx"), P()), check_vma=False
    )
```

```python
import functools
import math

import jax
import jax.numpy as jnp
from jax import lax
from jax.experimental import pallas as pl
from jax.experimental.pallas import tpu as pltpu
from jax.sharding import PartitionSpec as P

MESH = pl.DeviceIdType.MESH
F32, BF16 = jnp.float32, jnp.bfloat16
HD = 2560
TOK = 144
SEQ = 1152
NZ, NX, NY = 8, 4, 8
DEPTH = 128
ROWS = 320
BLOCK = 384
EXACT = lax.Precision.HIGHEST
SCALE = math.log2(math.e) / math.sqrt(DEPTH)
SPANS = ((0, 640), (384, 1024), (768, 1152))


def rows_by_rows(left, right, precision=None):
    return lax.dot_general(
        left, right, (((1,), (1,)), ((), ())), preferred_element_type=F32, precision=precision
    )


def kernel(
    q_in, k_in, v_in, fr_in, og_in, qp_in, er_in,
    basis, q_out,
    qkv, code, frames, dys, packed, probs, attn, og, qp, er, mem, tok,
    others, xs, ys, xs1, ys1, halves, psum, gram, grams, bpack, bs,
    part, send, got, ys2, zs2, ys3, zs3,
    in_sem, recv, sent, step_recv, step_sent, tail_recv, tail_sent,
):
    dp, z = lax.axis_index("dp"), lax.axis_index("ctx")
    c, y, x = dp % 2, (dp // 2) % NY, dp // (2 * NY)
    zpar = z % 2
    par = (z + c) % 2
    mate = z + 1 - 2 * zpar
    even = zpar == 0
    far = (4, 3, 5, 2, 6, 1, 7)
    z_peers = [(dp, (z + d) % NZ) for d in far]
    w = 2 * x + c
    w_peers = [(((x + d) % NX) * 2 * NY + 2 * y + t, z) for d in (2, 1, 3) for t in (c, 1 - c)]
    w_peers.append((dp + 1 - 2 * c, z))
    y_peers = [(x * 2 * NY + 2 * ((y + d) % NY) + c, z) for d in far]

    def remote(src, dst, ssem, rsem, to):
        return pltpu.make_async_remote_copy(
            src_ref=src, dst_ref=dst, send_sem=ssem, recv_sem=rsem, device_id=to, device_id_type=MESH
        )

    def drain(ref, sem):
        pltpu.make_async_copy(ref, ref, sem).wait()

    loads = [
        pltpu.make_async_copy(src, dst, in_sem.at[i])
        for i, (src, dst) in enumerate(((og_in, og), (qp_in, qp), (er_in, er)))
    ]
    for load in loads:
        load.start()

    everyone = z_peers + w_peers + y_peers
    barrier = pltpu.get_barrier_semaphore()
    for to in everyone:
        pl.semaphore_signal(barrier, inc=1, device_id=to, device_id_type=MESH)
    pl.semaphore_wait(barrier, len(everyone))

    own_rows = pl.ds(pl.multiple_of(z * TOK, 16), TOK)
    tensors = (k_in, q_in, v_in)

    def columns(slot, t):
        head = 5 * (t // 2) + (2 if slot == 0 else 3 * (t % 2) + slot - 1)
        return pl.ds(pl.multiple_of(head * DEPTH, DEPTH), DEPTH)

    def send_to(slot, i, steps):
        for d in steps:
            t = (z + d) % NZ
            source, target = tensors[i].at[:, columns(slot, t)], qkv.at[slot, i, own_rows]
            if d == 0:
                pltpu.make_async_copy(source, target, recv.at[slot, i]).start()
            else:
                remote(source, target, sent.at[slot, i], recv.at[slot, i], (dp, t)).start()

    def send_head(slot, i):
        if slot > 0:
            send_to(slot, i, far + (0,))
            return

        @pl.when(par == 0)
        def _():
            send_to(0, i, (4, 2, 6, 0))

        @pl.when(par == 1)
        def _():
            send_to(0, i, (3, 5, 1, 7))

    def left(slot, i):
        if slot > 0:
            drain(qkv.at[0, i, 0 : 7 * TOK], sent.at[slot, i])
            return

        @pl.when(par == 0)
        def _():
            drain(qkv.at[0, i, 0 : 3 * TOK], sent.at[0, i])

        @pl.when(par == 1)
        def _():
            drain(qkv.at[0, i, 0 : 4 * TOK], sent.at[0, i])

    send_head(0, 0)
    pltpu.make_async_copy(fr_in, frames.at[z], step_recv.at[5]).start()
    for to in z_peers:
        remote(fr_in, frames.at[z], tail_sent.at[0], step_recv.at[5], to).start()
    send_head(0, 1)
    send_head(0, 2)

    loads[0].wait()
    loads[1].wait()
    found = rows_by_rows(qp[...], og[...])
    packed[...] = jnp.zeros_like(packed)
    packed[0:32] = found[:, 0:DEPTH]
    packed[32:48, 0:16] = found[0:16, DEPTH:]
    packed[32:48, 16:32] = found[16:32, DEPTH:]
    dys[z] = packed[...].astype(BF16)
    for to in z_peers:
        remote(dys.at[z], dys.at[z], tail_sent.at[1], tail_recv.at[1], to).start()
    send_head(1, 0)

    loads[2].wait()
    head_row = pl.multiple_of(64 * zpar, 64)
    half_row = pl.multiple_of(256 * (1 - zpar), 64)
    halves[...] = jnp.zeros((32, DEPTH), F32)
    halves[:, 0:64] = rows_by_rows(qp[...], er[pl.ds(half_row, 64), :])
    mine = halves[...]
    mem[0] = jnp.where(even, mine, pltpu.roll(mine, 64, 1))
    remote(mem.at[0], others.at[0], step_sent.at[4], step_recv.at[4], (dp, mate)).start()
    for s in (1, 2):
        rows = pl.ds(pl.multiple_of(head_row + DEPTH * (s - 1), 64), DEPTH)
        mem[s] = rows_by_rows(qp[...], er[rows, :])
    tok[...] = jnp.zeros_like(tok)
    bpack[...] = jnp.zeros_like(bpack)
    gram[...] = jnp.zeros_like(gram)

    drain(frames, step_recv.at[5])
    number = lax.broadcasted_iota(jnp.int32, (16, TOK), 0)
    place = (
        lax.broadcasted_iota(jnp.int32, (16, DEPTH), 0) == lax.broadcasted_iota(jnp.int32, (16, DEPTH), 1)
    ).astype(F32)
    for j in range(NZ):
        row = jnp.broadcast_to(frames[j], (16, TOK))
        for i, value in enumerate((jnp.where(row == number, 1.0, 0.0), jnp.where(row > number, -1e30, 0.0))):
            code[i, j * TOK : (j + 1) * TOK, :] = lax.dot_general(
                value, place, (((0,), (0,)), ((), ())), preferred_element_type=F32
            ).astype(BF16)
    drain(dys.at[0:7], tail_recv.at[1])

    lane = lax.broadcasted_iota(jnp.int32, (32, DEPTH), 1)

    def attend(s):
        drain(qkv.at[s, 0], recv.at[s, 0])
        drain(qkv.at[s, 1], recv.at[s, 1])
        for first, reach in SPANS:
            queries = jnp.concatenate([qkv[s, 1, first : first + BLOCK, :], code[0, first : first + BLOCK, :]], axis=1)
            keys = jnp.concatenate([qkv[s, 0, 0:reach, :], code[1, 0:reach, :]], axis=1)
            scores = rows_by_rows(queries, keys)
            top = jnp.max(scores, axis=1, keepdims=True)
            probs[first : first + BLOCK, 0:reach] = jnp.exp2((scores - top) * SCALE).astype(BF16)
        drain(qkv.at[s, 2], recv.at[s, 2])
        for first, reach in SPANS:
            values = jnp.concatenate([qkv[s, 2, 0:reach, :], jnp.ones((reach, DEPTH), BF16)], axis=1)
            mixed = jnp.dot(probs[first : first + BLOCK, 0:reach], values, preferred_element_type=F32)
            attn[s, first : first + BLOCK, :] = (mixed[:, 0:DEPTH] / mixed[:, DEPTH:]).astype(BF16)
        total = jnp.zeros((32, DEPTH), F32)
        for j in range(NZ):
            main, rest = dys[j, 0:32, :], dys[j, 32:48, :].astype(F32)
            rest = jnp.concatenate([rest, pltpu.roll(rest, DEPTH - 16, 1)], axis=0)[:, 0:16].astype(BF16)
            total += jnp.dot(main, attn[s, j * TOK : j * TOK + DEPTH, :], preferred_element_type=F32)
            total += jnp.dot(rest, attn[s, j * TOK + DEPTH : (j + 1) * TOK, :], preferred_element_type=F32)
        tok[s] = total

    def over(blocks):
        total = blocks[0].astype(F32)
        for j in range(1, 8):
            total += blocks[j].astype(F32)
        return total

    def head(s, carry):
        @pl.when(s == 0)
        def _():
            for i, ahead in enumerate(((1, 1), (1, 2), (2, 0))):
                left(0, i)
                send_head(*ahead)

        @pl.when(s == 1)
        def _():
            left(1, 0)
            send_head(2, 1)

        @pl.when(jnp.logical_or(s > 0, par == 0))
        def _():
            attend(s)

        @pl.when(jnp.logical_and(s == 0, par == 0))
        def _():
            remote(tok.at[0], others.at[1], step_sent.at[3], step_recv.at[3], (dp, mate)).start()

        @pl.when(s == 1)
        def _():
            drain(others.at[0], step_recv.at[4])

            @pl.when(par == 1)
            def _():
                attn[0] = jnp.zeros((SEQ, DEPTH), BF16)
                drain(others.at[1], step_recv.at[3])
                tok[0] = others[1]

            xs[w, 0] = ((mem[0] + others[0]) + tok[0]).astype(BF16)
            xs[w, 1] = (mem[1] + tok[1]).astype(BF16)
            for to in w_peers:
                remote(xs.at[w], xs.at[w], step_sent.at[1], step_recv.at[1], to).start()
            left(1, 1)
            send_head(2, 2)
            drain(xs.at[0:7], step_recv.at[1])
            ys[y] = over(xs).astype(BF16)
            for to in y_peers:
                remote(ys.at[y], ys.at[y], step_sent.at[2], step_recv.at[2], to).start()

        return carry

    lax.fori_loop(0, 3, head, 0)

    xs1[w] = (mem[2] + tok[2]).astype(BF16)
    for to in w_peers:
        remote(xs1.at[w], xs1.at[w], tail_sent.at[5], tail_recv.at[5], to).start()
    drain(ys.at[0:7], step_recv.at[2])
    psum[0:2] = over(ys)
    drain(xs1.at[0:7], tail_recv.at[5])
    ys1[y] = over(xs1).astype(BF16)
    for to in y_peers:
        remote(ys1.at[y], ys1.at[y], step_sent.at[0], step_recv.at[0], to).start()
    drain(ys1.at[0:7], step_recv.at[0])
    psum[2] = over(ys1)

    own = jnp.where((lane < 64) == even, psum[0], 0.0)
    gram[:, 0:32] = rows_by_rows(own, own, EXACT)
    for s in (1, 2):
        gram[:, 0:32] += rows_by_rows(psum[s], psum[s], EXACT)
    folded = gram[0:8]
    for j in range(1, 4):
        folded += pltpu.roll(gram[8 * j : 8 * j + 8], 32 * j, 1)
    grams[z] = folded
    for to in z_peers:
        remote(grams.at[z], grams.at[z], tail_sent.at[2], tail_recv.at[2], to).start()

    rows = jnp.concatenate([psum[0], psum[1], psum[2]], axis=1)
    high = rows.astype(BF16)
    both = jnp.concatenate([high, (rows - high.astype(F32)).astype(BF16)], axis=0)
    for d in far + (0,):
        t = (z + d) % NZ
        first = pl.multiple_of(t * TOK, 16)
        for count, start in ((DEPTH, 0), (TOK - DEPTH, DEPTH)):
            heads = [attn[s, pl.ds(first + start, count), :] for s in range(3)]
            found = rows_by_rows(both, jnp.concatenate(heads, axis=1))
            found = found[0:32] + found[32:64]
            if start == 0:
                bpack[t, 0:32] = found
            else:
                for i in range(4):
                    bpack[t, 32:40, 16 * i : 16 * i + 16] = found[8 * i : 8 * i + 8]
        if d > 0:
            remote(bpack.at[t], bs.at[z], tail_sent.at[3], tail_recv.at[3], (dp, t)).start()
        else:
            bs[z] = bpack[z]

    drain(grams.at[0:7], tail_recv.at[2])
    folded = grams[0]
    for j in range(1, NZ):
        folded += grams[j]
    line = lax.broadcasted_iota(jnp.int32, (32, DEPTH), 0)
    work = jnp.concatenate([folded] + [pltpu.roll(folded, DEPTH - 32 * j, 1) for j in range(1, 4)], axis=0)
    work = jnp.where(lane < 32, work, jnp.where(lane - 32 == line, 1.0, 0.0))
    for j in range(32):
        pivot = work[j : j + 1, j : j + 1]
        scale = lax.rsqrt(pivot)
        row = work[j : j + 1, :] * scale
        column = jnp.where(line[:, 0:1] > j, work[:, j : j + 1] * scale, 0.0)
        work = jnp.where(line == j, row, work - column * row)
    inverse = pltpu.roll(work, DEPTH - 32, 1)[:, 0:32]

    units = [jnp.dot(inverse, psum[s], preferred_element_type=F32, precision=EXACT) for s in range(3)]
    middle_unit, first_unit, second_unit = [unit * math.sqrt(HD) for unit in units]
    first_turned, second_turned = pltpu.roll(first_unit, 64, 1), pltpu.roll(second_unit, 64, 1)
    low = lane < 64
    middle_turned = pltpu.roll(middle_unit, 64, 1)
    basis[:, 0:128] = jnp.where(even, first_unit, jnp.where(low, middle_turned, first_turned))
    basis[:, 128:256] = jnp.where(even, second_unit, jnp.where(low, first_turned, second_turned))
    basis[:, 256:384] = jnp.where(even, middle_unit, second_turned)

    wide = 640
    units[0] = jnp.where(even, units[0], pltpu.roll(units[0], 64, 1))
    middle_bf, first_bf, second_bf = [unit.astype(BF16) for unit in units]
    for j in range(4):
        cols = slice(wide * j, wide * (j + 1))
        part[:, cols] = (
            jnp.dot(first_bf, er[pl.ds(head_row, DEPTH), cols], preferred_element_type=F32)
            + jnp.dot(second_bf, er[pl.ds(pl.multiple_of(head_row + DEPTH, 64), DEPTH), cols], preferred_element_type=F32)
            + jnp.dot(middle_bf[:, 0:64], er[pl.ds(half_row, 64), cols], preferred_element_type=F32)
        )

    drain(bs.at[0:7], tail_recv.at[3])
    summed = bs[0]
    for j in range(1, NZ):
        summed += bs[j]
    rest = jnp.concatenate([summed[32:40, 16 * i : 16 * i + 16] for i in range(4)], axis=0)
    a_proj = jnp.dot(inverse, summed[0:32], preferred_element_type=F32, precision=EXACT).astype(BF16)
    a_rest = jnp.dot(inverse, rest, preferred_element_type=F32, precision=EXACT).astype(BF16)
    for j in range(4):
        cols = slice(wide * j, wide * (j + 1))
        found = part[:, cols] + jnp.dot(a_proj, og[0:DEPTH, cols], preferred_element_type=F32)
        found += jnp.dot(a_rest, og[DEPTH:TOK, cols], preferred_element_type=F32)
        for r in range(2):
            place = 4 * r + j
            send[place] = found[16 * r : 16 * r + 16].astype(BF16)

            @pl.when(w == place)
            def _():
                got[place] = send[place]

            @pl.when(w != place)
            def _():
                to = ((place // 2) * 2 * NY + 2 * y + place % 2, z)
                remote(send.at[place], got.at[w], tail_sent.at[4], tail_recv.at[4], to).start()

    drain(got.at[0:7], tail_recv.at[4])
    total = over(got).astype(BF16)
    ys2[y] = total[:, 0:384]
    zs3[z] = total[:, 384:640]
    for one, two in zip(y_peers, z_peers):
        remote(ys2.at[y], ys2.at[y], tail_sent.at[7], tail_recv.at[7], one).start()
        remote(zs3.at[z], zs3.at[z], tail_sent.at[9], tail_recv.at[9], two).start()
    drain(ys2.at[0:7], tail_recv.at[7])
    zs2[z] = over(ys2).astype(BF16)
    drain(zs3.at[0:7], tail_recv.at[9])
    ys3[y] = over(zs3).astype(BF16)
    for one, two in zip(y_peers, z_peers):
        remote(zs2.at[z], zs2.at[z], tail_sent.at[6], tail_recv.at[6], two).start()
        remote(ys3.at[y], ys3.at[y], tail_sent.at[10], tail_recv.at[10], one).start()
    drain(zs2.at[0:7], tail_recv.at[6])
    q_out[w, :, 0:384] = over(zs2).astype(BF16)
    drain(ys3.at[0:7], tail_recv.at[10])
    q_out[w, :, 384:640] = over(ys3).astype(BF16)
    for to in w_peers:
        remote(q_out.at[w], q_out.at[w], tail_sent.at[8], tail_recv.at[8], to).start()
    drain(q_out.at[0:7], tail_recv.at[8])

    for s, i in ((1, 2), (2, 0), (2, 1), (2, 2)):
        left(s, i)

    @pl.when(par == 0)
    def _():
        drain(others.at[1], step_sent.at[3])

    drain(mem.at[0], step_sent.at[4])
    drain(xs1.at[0:7], tail_sent.at[5])
    drain(ys1.at[0:7], step_sent.at[0])
    drain(xs.at[0:7], step_sent.at[1])
    drain(ys.at[0:7], step_sent.at[2])
    drain(frames.at[0:7], tail_sent.at[0])
    drain(dys.at[0:7], tail_sent.at[1])
    drain(grams.at[0:7], tail_sent.at[2])
    drain(bs.at[0:7], tail_sent.at[3])
    drain(got.at[0:7], tail_sent.at[4])
    drain(zs2.at[0:7], tail_sent.at[6])
    drain(zs3.at[0:7], tail_sent.at[9])
    drain(ys3.at[0:7], tail_sent.at[10])
    drain(ys2.at[0:7], tail_sent.at[7])
    drain(q_out.at[0:7], tail_sent.at[8])


def finish(wide_basis, parts, basis, q_out):
    basis[...] = wide_basis[:, 0:ROWS]
    for j in range(NZ):
        r, g = j // 4, j % 4
        q_out[16 * r : 16 * r + 16, 640 * g : 640 * (g + 1)] = parts[j].astype(F32) * (1.0 / 64)


def body(queries, keys, values, frame_ids, out_grad, q_prev, error):
    vmem, dma = pltpu.VMEM, pltpu.SemaphoreType.DMA
    basis, q_factor = pl.pallas_call(
        kernel,
        out_shape=(jax.ShapeDtypeStruct((32, 384), F32), jax.ShapeDtypeStruct((NZ, 16, 640), BF16)),
        in_specs=[pl.BlockSpec(memory_space=pl.ANY)] * 7,
        out_specs=(pl.BlockSpec(memory_space=vmem), pl.BlockSpec(memory_space=vmem)),
        scratch_shapes=[
            vmem((3, 3, SEQ, DEPTH), BF16),
            vmem((2, SEQ, DEPTH), BF16),
            vmem((NZ, 1, TOK), jnp.int32),
            vmem((NZ, 48, DEPTH), BF16),
            vmem((48, DEPTH), F32),
            vmem((SEQ, SEQ), BF16),
            vmem((3, SEQ, DEPTH), BF16),
            vmem((TOK, HD), BF16),
            vmem((32, HD), BF16),
            vmem((ROWS, HD), BF16),
            vmem((3, 32, DEPTH), F32),
            vmem((3, 32, DEPTH), F32),
            vmem((2, 32, DEPTH), F32),
            vmem((8, 2, 32, DEPTH), BF16),
            vmem((NY, 2, 32, DEPTH), BF16),
            vmem((8, 32, DEPTH), BF16),
            vmem((NY, 32, DEPTH), BF16),
            vmem((32, DEPTH), F32),
            vmem((3, 32, DEPTH), F32),
            vmem((32, DEPTH), F32),
            vmem((NZ, 8, DEPTH), F32),
            vmem((NZ, 40, DEPTH), F32),
            vmem((NZ, 40, DEPTH), F32),
            vmem((32, HD), F32),
            vmem((NZ, 16, 640), BF16),
            vmem((NZ, 16, 640), BF16),
            vmem((NY, 16, 384), BF16),
            vmem((NZ, 16, 384), BF16),
            vmem((NY, 16, 256), BF16),
            vmem((NZ, 16, 256), BF16),
            dma((3,)),
            dma((3, 3)),
            dma((3, 3)),
            dma((6,)),
            dma((6,)),
            dma((11,)),
            dma((11,)),
        ],
        compiler_params=pltpu.CompilerParams(
            collective_id=0, has_side_effects=True, vmem_limit_bytes=56 * 1024 * 1024
        ),
    )(queries[0], keys[0], values[0], frame_ids, out_grad[0], q_prev, error[0])
    return pl.pallas_call(
        finish,
        out_shape=(jax.ShapeDtypeStruct((32, ROWS), F32), jax.ShapeDtypeStruct((32, HD), F32)),
    )(basis, q_factor)


def solution(mesh):
    placed = (
        P("dp", "ctx", None),
        P("dp", "ctx", None),
        P("dp", "ctx", None),
        P("dp", "ctx"),
        P("dp", "ctx", None),
        P(),
        P("dp", "ctx", None),
    )
    return jax.shard_map(
        body, mesh=mesh, in_specs=placed, out_specs=(P(None, "ctx"), P()), check_vma=False
    )
```
